32 devices in a mesh: sample: 2 (over x), space: 16 (over z, y, core).
Axes of the slice: x: 2, y: 2, z: 4, core: 2. Of those that a mesh axis runs over, the one named last changes fastest.
Arguments:
- volumes: bfloat16 [2, 64, 16, 64, 128], P('sample', 'space'), may hold values from -6 to 6
- fine_kernel: bfloat16 [27, 128, 128], replicated, may hold values from -0.109375 to 0.109375
- coarse_kernel: bfloat16 [27, 128, 256], replicated, may hold values from -0.109375 to 0.109375
- cotangent: bfloat16 [2, 32, 8, 32, 256], P('sample', 'space'), may hold values from -6 to 6
Outputs:
- coarse_out: bfloat16 [2, 32, 8, 32, 256], P('sample', 'space')
- fine_grad: float32 [128, 3456], P('space')
- coarse_grad: float32 [256, 3456], P('space')
The draws below stay inside these ranges and needn't reach their ends.
All inputs are finite; a program needn't handle non-finite values.
Results may differ from the reference program's by a relative error of at most 0.014.
Values may be sent and summed in bfloat16 or wider, within the bound.
No kernel may reach another device: no remote copies, remote signals or barrier semaphores. Data moves between devices by JAX's collectives and lax.ppermute only.
A program may use at most 128 MiB of HBM per device.

```python
import jax
import jax.numpy as jnp
from jax import lax

C1 = 128
C2 = 256
NY = 16
NZ = 64
SAMPLES = 2
NX = 64


def level_of(rng, extent, split, low, top_value):
    loudness, own = 1.0, jax.random.fold_in(rng, 6)
    for axis_at, shards_of in split:
        heights = jnp.exp(jax.random.uniform(jax.random.fold_in(own, axis_at), (shards_of,), jnp.float32, low / len(split), top_value / len(split)))
        loudness = loudness * jnp.repeat(heights, extent[axis_at] // shards_of).reshape([-1 if axis == axis_at else 1 for axis in range(len(extent))])
    return loudness


def normal_values(rng, shape, width, reach, shards=(), kind=jnp.bfloat16):
    factor_of = level_of(rng, shape, shards, -0.22, 0.18) if shards else 1.0
    result = jax.random.normal(rng, shape, jnp.float32) * width * factor_of
    return jnp.minimum(jnp.maximum(result, -reach), reach).astype(kind)


def setup_inputs(seed: int = 0) -> dict:
    splits = jax.random.split(jax.random.key(seed), 5)
    volumes = normal_values(splits[0], (SAMPLES, NX, NY, NZ, C1), 1.0, 6.0, ((0, 2), (1, 16)))
    fine_kernel = normal_values(splits[1], (27, C1, C1), (27 * C1) ** -0.5, 0.109375)
    coarse_kernel = normal_values(splits[2], (27, C1, C2), (27 * C1) ** -0.5, 0.109375)
    cotangent = normal_values(splits[3], (SAMPLES, NX // 2, NY // 2, NZ // 2, C2), 1.0, 6.0, ((0, 2), (1, 16)))
    return dict(volumes=volumes, fine_kernel=fine_kernel, coarse_kernel=coarse_kernel, cotangent=cotangent)


def silu_slope(value):
    sig = jax.nn.sigmoid(value)
    return sig * (1.0 + value * (1.0 - sig))


def shifted(padded, tap, shape):
    first = (tap // 9).astype(jnp.int32)
    second = ((tap // 3) % 3).astype(jnp.int32)
    third = (tap % 3).astype(jnp.int32)
    anchor = jnp.zeros((), jnp.int32)
    piece = lax.dynamic_slice(padded, (first, second, third, anchor), (shape[0], shape[1], shape[2], padded.shape[3]))
    return piece.reshape(-1, padded.shape[-1])


def tap_list():
    return jnp.arange(27, dtype=jnp.int32)


def forward_taps(field, kernel):
    shape = field.shape[:3]
    padded = jnp.pad(field, ((1, 1), (1, 1), (1, 1), (0, 0)))
    start = jnp.zeros((shape[0] * shape[1] * shape[2], kernel.shape[2]), jnp.float32)

    def step(total, inputs):
        tap, weight = inputs
        total = total + jnp.dot(shifted(padded, tap, shape), weight, preferred_element_type=jnp.float32)
        return total, None

    total, unused = lax.scan(step, start, (tap_list(), kernel))
    return total, padded


def backward_taps(delta, kernel):
    shape = delta.shape[:3]
    padded = jnp.pad(delta, ((1, 1), (1, 1), (1, 1), (0, 0)))
    start = jnp.zeros((shape[0] * shape[1] * shape[2], kernel.shape[1]), jnp.float32)

    def step(total, inputs):
        tap, weight = inputs
        flipped = (26 - tap).astype(jnp.int32)
        total = total + lax.dot_general(shifted(padded, flipped, shape), weight, (((1,), (1,)), ((), ())), preferred_element_type=jnp.float32)
        return total, None

    total, unused = lax.scan(step, start, (tap_list(), kernel))
    return total


def kernel_term(delta_rows, padded, shape):
    def step(carry, tap):
        piece = lax.dot_general(delta_rows, shifted(padded, tap, shape), (((0,), (0,)), ((), ())), preferred_element_type=jnp.float32)
        return carry, piece

    unused, pieces = lax.scan(step, jnp.zeros((), jnp.float32), tap_list())
    return jnp.moveaxis(pieces, 0, 1).reshape(pieces.shape[1], -1)


def reference(volumes, fine_kernel, coarse_kernel, cotangent):
    outputs = []
    fine_total = jnp.zeros((fine_kernel.shape[2], 27 * fine_kernel.shape[1]), jnp.float32)
    coarse_total = jnp.zeros((coarse_kernel.shape[2], 27 * coarse_kernel.shape[1]), jnp.float32)
    for index in range(volumes.shape[0]):
        field = volumes[index]
        fx, fy, fz, chan = field.shape
        fine_pre, fine_pad = forward_taps(field, fine_kernel)
        fine_act = jax.nn.silu(fine_pre).astype(jnp.bfloat16)
        blocks = fine_act.astype(jnp.float32).reshape(fx // 2, 2, fy // 2, 2, fz // 2, 2, chan)
        pooled = jnp.mean(blocks, axis=(1, 3, 5)).astype(jnp.bfloat16)
        coarse_pre, coarse_pad = forward_taps(pooled, coarse_kernel)
        outputs.append(jax.nn.silu(coarse_pre).astype(jnp.bfloat16).reshape(fx // 2, fy // 2, fz // 2, -1))
        grad_rows = cotangent[index].reshape(-1, coarse_kernel.shape[2]).astype(jnp.float32)
        coarse_delta = (grad_rows * silu_slope(coarse_pre)).astype(jnp.bfloat16)
        pooled_grad = backward_taps(coarse_delta.reshape(fx // 2, fy // 2, fz // 2, -1), coarse_kernel).astype(jnp.bfloat16)
        spread = pooled_grad.astype(jnp.float32).reshape(fx // 2, fy // 2, fz // 2, chan) / 8.0
        spread = jnp.repeat(jnp.repeat(jnp.repeat(spread, 2, axis=0), 2, axis=1), 2, axis=2)
        fine_delta = (spread.reshape(-1, chan) * silu_slope(fine_pre)).astype(jnp.bfloat16)
        fine_total = fine_total + kernel_term(fine_delta, fine_pad, (fx, fy, fz))
        coarse_total = coarse_total + kernel_term(coarse_delta, coarse_pad, (fx // 2, fy // 2, fz // 2))
    return jnp.stack(outputs), fine_total, coarse_total
```

```python
import functools

import jax
import jax.numpy as jnp
from jax import lax
from jax.experimental import pallas as pl
from jax.experimental.pallas import tpu as pltpu
from jax.sharding import PartitionSpec as P

F32 = jnp.float32
BF16 = jnp.bfloat16
VMEM = pl.BlockSpec(memory_space=pltpu.VMEM)
SMEM = pl.BlockSpec(memory_space=pltpu.SMEM)


def size_of(shapes):
    total = 0
    for item in shapes:
        count = jnp.dtype(item.dtype).itemsize
        for extent in item.shape:
            count *= extent
        total += count
    return total


def kernel_call(body, operands, outs, scratch, flops, limit, scalars=0):
    cost = pl.CostEstimate(
        flops=flops, bytes_accessed=size_of(operands) + size_of(outs), transcendentals=0
    )
    specs = [SMEM] * scalars + [VMEM] * (len(operands) - scalars)
    return pl.pallas_call(
        body,
        out_shape=outs,
        in_specs=specs,
        out_specs=[VMEM] * len(outs),
        scratch_shapes=scratch,
        cost_estimate=cost,
        compiler_params=pltpu.CompilerParams(vmem_limit_bytes=limit * 2**20),
    )(*operands)


def neighbours(first, last, axis):
    count = lax.axis_size(axis)
    up = [(i, i + 1) for i in range(count - 1)]
    down = [(i + 1, i) for i in range(count - 1)]
    return lax.ppermute(last, axis, up), lax.ppermute(first, axis, down)


def silu_slope(value, sig):
    return sig * (1.0 + value * (1.0 - sig))


def three_shifts(value):
    depth = value.shape[1]
    at = lax.broadcasted_iota(jnp.int32, value.shape, 1)
    lower = jnp.where(at == 0, 0.0, pltpu.roll(value, 1, 1))
    upper = jnp.where(at == depth - 1, 0.0, pltpu.roll(value, depth - 1, 1))
    return lower, value, upper


def tap_dot(left, right):
    return lax.dot_general(left, right, (((0,), (0,)), ((), ())), preferred_element_type=F32)


def fine_forward(before, own, after, kernel, wide6, pooled, slope, weights, sums):
    planes, fy, fz, chan = own.shape
    half = fy // 2
    for s in range(2):
        for r in range(2):
            for q in range(2):
                b = 2 * s + r - q
                for a in range(3):
                    place = (a, s, pl.ds(r * 3 * chan, 3 * chan), pl.ds(q * chan, chan))
                    if 0 <= b <= 2:
                        weights[place] = kernel[3 * a + b]
                    else:
                        weights[place] = jnp.zeros((3 * chan, chan), BF16)

    def spread(source, plane, target):
        zero = jnp.zeros((fz, 3 * chan), BF16)
        wide6[target, 0, :, 0 : 3 * chan] = zero
        wide6[target, half, :, 3 * chan : 6 * chan] = zero

        @pl.loop(0, half)
        def _(j):
            for odd in range(2):
                row = source[plane, pl.ds(2 * j + odd, 1)].astype(F32)
                for c, piece in enumerate(three_shifts(row)):
                    lane = (1 - odd) * 3 * chan + c * chan
                    wide6[target, pl.ds(j + odd, 1), :, lane : lane + chan] = piece.astype(BF16)

    spread(before, 0, 0)
    spread(after, 0, planes + 1)

    @pl.loop(0, planes)
    def _(p):
        spread(own, p, p + 1)

    @pl.loop(0, planes // 2)
    def _(pair):
        for u in range(2):
            p = 2 * pair + u
            pre = None
            for a in range(3):
                for s in range(2):
                    rows = wide6[p + a, s : s + half].reshape(half * fz, 6 * chan)
                    term = jnp.dot(rows, weights[a, s], preferred_element_type=F32)
                    pre = term if pre is None else pre + term
            sig = jax.nn.sigmoid(pre)
            act = (pre * sig).astype(BF16).astype(F32)
            slope[p] = silu_slope(pre, sig).astype(BF16).reshape(half, fz, 2 * chan)
            act = (act[:, :chan] + act[:, chan:]).reshape(half, fz, chan)
            if u == 0:
                sums[...] = act
            else:
                sums[...] += act
        both = sums[:, pl.ds(0, fz // 2, stride=2), :] + sums[:, pl.ds(1, fz // 2, stride=2), :]
        pooled[pair] = (both * 0.125).astype(BF16)


def fill_wide3(target, plane, value):
    rows, depth, chan = value.shape
    zero = jnp.zeros((depth, 3 * chan), BF16)
    target[plane, 0] = zero
    target[plane, rows + 1] = zero
    for c, piece in enumerate(three_shifts(value.astype(F32))):
        target[plane, 1 : rows + 1, :, c * chan : (c + 1) * chan] = piece.astype(BF16)


def coarse_forward(before, own, after, kernel, cotangent, wide3, out, delta):
    planes, cy, cz, chan = own.shape
    wide = kernel.shape[-1]
    fill_wide3(wide3, 0, before[0])
    for p in range(planes):
        fill_wide3(wide3, p + 1, own[p])
    fill_wide3(wide3, planes + 1, after[0])
    for p in range(planes):
        pre = None
        for a in range(3):
            for b in range(3):
                rows = wide3[p + a, b : b + cy].reshape(cy * cz, 3 * chan)
                term = jnp.dot(rows, kernel[3 * a + b], preferred_element_type=F32)
                pre = term if pre is None else pre + term
        sig = jax.nn.sigmoid(pre)
        out[p] = (pre * sig).astype(BF16).reshape(cy, cz, wide)
        grad = cotangent[p].reshape(cy * cz, wide).astype(F32) * silu_slope(pre, sig)
        delta[p] = grad.astype(BF16).reshape(cy, cz, wide)


def put_term(term, lane, place, keep, send, order):
    if send is None:
        keep[:, lane : lane + term.shape[1]] = term.astype(BF16)
        return
    here = place[0] == 0
    rows = term.shape[0] // (2 * len(order))
    for at, owner in enumerate(order):
        low = term[owner * rows : (owner + 1) * rows]
        high = term[(owner + 1) * rows : (owner + 2) * rows]
        keep[at, :, lane : lane + term.shape[1]] = jnp.where(here, low, high).astype(BF16)
        send[at, :, lane : lane + term.shape[1]] = jnp.where(here, high, low).astype(BF16)


def coarse_terms(place, wide3, delta, keep, send=None, *, order):
    planes, cy, cz, wide = delta.shape
    span = wide3.shape[-1]
    rows = delta[...].reshape(planes * cy * cz, wide)
    for a in range(3):
        for b in range(3):
            piece = wide3[a : a + planes, b : b + cy].reshape(planes * cy * cz, span)
            put_term(tap_dot(rows, piece), (3 * a + b) * span, place, keep, send, order)


def fine_backward(before, own, after, kernel, slope, delta, wide3, spread):
    planes, cy, cz, wide = own.shape
    chan = kernel.shape[1]
    fill_wide3(wide3, 0, before[0])
    for p in range(planes):
        fill_wide3(wide3, p + 1, own[p])
    fill_wide3(wide3, planes + 1, after[0])
    for p in range(planes):
        grad = None
        for a in range(3):
            for b in range(3):
                for c in range(3):
                    rows = wide3[p + a, b : b + cy, :, c * wide : (c + 1) * wide]
                    term = lax.dot_general(
                        rows.reshape(cy * cz, wide),
                        kernel[26 - (9 * a + 3 * b + c)],
                        (((1,), (1,)), ((), ())),
                        preferred_element_type=F32,
                    )
                    grad = term if grad is None else grad + term
        grad = grad.astype(BF16).astype(F32).reshape(cy, cz, chan) * 0.125
        spread[:, pl.ds(0, cz, stride=2), :] = grad
        spread[:, pl.ds(1, cz, stride=2), :] = grad
        near = spread[...]
        both = jnp.concatenate([near, near], axis=-1)
        for u in range(2):
            delta[2 * p + u] = (both * slope[2 * p + u].astype(F32)).astype(BF16)


def fine_terms(place, wide6, delta, keep, send=None, *, order):
    planes, half, fz, double = delta.shape
    chan = double // 2
    for a in range(3):
        for b in range(3):
            total = None
            for p in range(planes):
                for q in range(2):
                    pair, parity = ((q + b) // 2, (q + b) % 2)
                    rows = delta[p, :, :, q * chan : (q + 1) * chan].reshape(half * fz, chan)
                    piece = wide6[
                        p + a, pair : pair + half, :, parity * 3 * chan : (parity + 1) * 3 * chan
                    ].reshape(half * fz, 3 * chan)
                    term = tap_dot(rows, piece)
                    total = term if total is None else total + term
            put_term(total, (3 * a + b) * 3 * chan, place, keep, send, order)


def swap(value, axis, bit):
    count = lax.axis_size(axis)
    return lax.ppermute(value, axis, [(i, i ^ bit) for i in range(count)])


def exchange_order(count):
    bits = count.bit_length() - 1
    order = []
    for at in range(count // 2):
        owner = 0
        for k in range(bits - 1):
            owner |= ((at >> (bits - 2 - k)) & 1) << (k + 1)
        order.append(owner)
    return order


def sum_terms(body, wide6, delta, rows, columns, flops, limit):
    count = lax.axis_size("space")
    me = lax.axis_index("space")
    bits = count.bit_length() - 1
    owned = rows // count
    place = jnp.reshape(me % 2, (1,)).astype(jnp.int32)
    order = exchange_order(count)
    direct = owned % 8 == 0
    if direct:
        shape = jax.ShapeDtypeStruct((count // 2, owned, columns), BF16)
        outs = [shape, shape]
    else:
        outs = [jax.ShapeDtypeStruct((rows, columns), BF16)]
    result = kernel_call(
        functools.partial(body, order=order),
        [place, wide6, delta],
        outs,
        [],
        flops,
        limit,
        scalars=1,
    )
    if direct:
        keep, send = result
    else:
        parts = result[0].reshape((2,) * bits + (owned, columns))
        parts = parts.transpose(tuple(reversed(range(bits))) + (bits, bits + 1))
        keep = lax.dynamic_index_in_dim(parts, me % 2, 0, keepdims=False)
        send = lax.dynamic_index_in_dim(parts, 1 - me % 2, 0, keepdims=False)
    total = keep.astype(F32) + swap(send, "space", 1).astype(F32)
    for k in range(1, bits):
        total = total.reshape(2, -1, owned, columns)
        mine = (me >> k) & 1
        send = lax.dynamic_index_in_dim(total, 1 - mine, 0, keepdims=False).astype(BF16)
        keep = lax.dynamic_index_in_dim(total, mine, 0, keepdims=False)
        total = keep + swap(send, "space", 1 << k).astype(F32)
    total = total.reshape(owned, columns)
    samples = lax.axis_size("sample")
    base = total.astype(BF16)
    if samples != 2:
        return lax.psum(base, "sample").astype(F32)
    return base.astype(F32) + swap(base, "sample", 1).astype(F32)


def shards(volumes, fine_kernel, coarse_kernel, cotangent):
    planes, fy, fz, chan = volumes.shape[1:]
    wide = coarse_kernel.shape[2]
    cp, cy, cz = (planes // 2, fy // 2, fz // 2)
    half = fy // 2
    shape = jax.ShapeDtypeStruct
    x = volumes[0]
    cells, few = (planes * fy * fz, cp * cy * cz)
    fine_flops, coarse_flops = (54 * cells * chan * chan, 54 * few * chan * wide)

    before, after = neighbours(x[:1], x[-1:], "space")
    wide6, pooled, slope = kernel_call(
        fine_forward,
        [before, x, after, fine_kernel.reshape(9, 3 * chan, chan)],
        [
            shape((planes + 2, half + 1, fz, 6 * chan), BF16),
            shape((cp, cy, cz, chan), BF16),
            shape((planes, half, fz, 2 * chan), BF16),
        ],
        [pltpu.VMEM((3, 2, 6 * chan, 2 * chan), BF16), pltpu.VMEM((half, fz, chan), F32)],
        fine_flops,
        24,
    )
    before, after = neighbours(pooled[:1], pooled[-1:], "space")
    wide3, out, coarse_delta = kernel_call(
        coarse_forward,
        [before, pooled, after, coarse_kernel.reshape(9, 3 * chan, wide), cotangent[0]],
        [
            shape((cp + 2, cy + 2, cz, 3 * chan), BF16),
            shape((cp, cy, cz, wide), BF16),
            shape((cp, cy, cz, wide), BF16),
        ],
        [],
        coarse_flops,
        16,
    )
    before, after = neighbours(coarse_delta[:1], coarse_delta[-1:], "space")
    coarse_grad = sum_terms(
        coarse_terms, wide3, coarse_delta, wide, 27 * chan, coarse_flops, 16
    )
    (fine_delta,) = kernel_call(
        fine_backward,
        [before, coarse_delta, after, coarse_kernel, slope],
        [shape((planes, half, fz, 2 * chan), BF16)],
        [pltpu.VMEM((cp + 2, cy + 2, cz, 3 * wide), BF16), pltpu.VMEM((cy, fz, chan), F32)],
        coarse_flops,
        16,
    )
    fine_grad = sum_terms(fine_terms, wide6, fine_delta, chan, 27 * chan, fine_flops, 24)
    return (out[None], fine_grad, coarse_grad)


def solution(mesh):
    placed = (
        P("sample", "space", None, None, None),
        P(),
        P(),
        P("sample", "space", None, None, None),
    )
    return jax.shard_map(
        shards,
        mesh=mesh,
        in_specs=placed,
        out_specs=(P("sample", "space", None, None, None), P("space", None), P("space", None)),
        check_vma=False,
    )
```

```python
import functools

import jax
import jax.numpy as jnp
from jax import lax
from jax.experimental import pallas as pl
from jax.experimental.pallas import tpu as pltpu
from jax.sharding import PartitionSpec as P

F32 = jnp.float32
BF16 = jnp.bfloat16
VMEM = pl.BlockSpec(memory_space=pltpu.VMEM)
SMEM = pl.BlockSpec(memory_space=pltpu.SMEM)


def size_of(shapes):
    total = 0
    for item in shapes:
        count = jnp.dtype(item.dtype).itemsize
        for extent in item.shape:
            count *= extent
        total += count
    return total


def kernel_call(body, operands, outs, scratch, flops, limit, scalars=0, after=()):
    cost = pl.CostEstimate(
        flops=flops, bytes_accessed=size_of(operands) + size_of(outs), transcendentals=0
    )
    used, extra = (len(operands), len(after))
    specs = [SMEM] * scalars + [VMEM] * (used - scalars)
    specs += [pl.BlockSpec(memory_space=pl.ANY)] * extra

    def inner(*refs):
        body(*refs[:used], *refs[used + extra :])

    return pl.pallas_call(
        inner,
        out_shape=outs,
        in_specs=specs,
        out_specs=[VMEM] * len(outs),
        scratch_shapes=scratch,
        cost_estimate=cost,
        compiler_params=pltpu.CompilerParams(vmem_limit_bytes=limit * 2**20),
    )(*operands, *after)


def exchange(to_pair, to_next):
    count = lax.axis_size("space")
    pair = [(i, i ^ 1) for i in range(count) if i ^ 1 < count]
    odd = [i for i in range(1, count - 1, 2)]
    across = [(i, i + 1) for i in odd] + [(i + 1, i) for i in odd]
    return lax.ppermute(to_pair, "space", pair), lax.ppermute(to_next, "space", across)


def silu_slope(value, sig):
    return sig * (1.0 + value * (1.0 - sig))


def three_shifts(value):
    depth = value.shape[1]
    at = lax.broadcasted_iota(jnp.int32, value.shape, 1)
    lower = jnp.where(at == 0, 0.0, pltpu.roll(value, 1, 1))
    upper = jnp.where(at == depth - 1, 0.0, pltpu.roll(value, depth - 1, 1))
    return lower, value, upper


def facing(place, edge, from_pair, from_next):
    return jnp.where(place[0] != edge, from_pair.astype(F32), from_next.astype(F32))


def send_planes(place, first, last, to_pair, to_next):
    even = place[0] == 0
    first, last = (first.astype(F32), last.astype(F32))
    to_pair[0] = jnp.where(even, last, first).astype(BF16)
    to_next[0] = jnp.where(even, first, last).astype(BF16)


def dot(left, right):
    return jnp.dot(left, right, preferred_element_type=F32)


def tap_dot(left, right):
    return lax.dot_general(left, right, (((0,), (0,)), ((), ())), preferred_element_type=F32)


def plus(total, term):
    return term if total is None else total + term


def fill_wide6(target, plane, row_of):
    half = target.shape[1] - 1
    depth, lanes = target.shape[2:]
    three = lanes // 2
    zero = jnp.zeros((depth, three), BF16)
    target[plane, 0, :, 0:three] = zero
    target[plane, half, :, three:lanes] = zero
    for y in range(2 * half):
        pair, parity = ((y + 1) // 2, (y + 1) % 2)
        for c, piece in enumerate(three_shifts(row_of(y))):
            lane = parity * three + c * (three // 3)
            target[plane, pair : pair + 1, :, lane : lane + three // 3] = piece.astype(BF16)


def fill_wide3(target, plane, value):
    rows, depth, chan = value.shape
    zero = jnp.zeros((depth, 3 * chan), BF16)
    target[plane, 0] = zero
    target[plane, rows + 1] = zero
    for c, piece in enumerate(three_shifts(value)):
        target[plane, 1 : rows + 1, :, c * chan : (c + 1) * chan] = piece.astype(BF16)


def fine_conv(wide6, plane, weights, a):
    half = wide6.shape[1] - 1
    total = None
    for s in range(2):
        rows = wide6[plane, s : s + half].reshape(half * wide6.shape[2], wide6.shape[3])
        total = plus(total, dot(rows, weights[a, s]))
    return total


def fine_finish(pre, half, depth):
    chan = pre.shape[1] // 2
    sig = jax.nn.sigmoid(pre)
    act = (pre * sig).astype(BF16).astype(F32)
    slope = silu_slope(pre, sig).astype(BF16).reshape(half, depth, 2 * chan)
    return (act[:, :chan] + act[:, chan:]).reshape(half, depth, chan), slope


def fine_inner(own, kernel, wide6, weights, edge, act, slope):
    planes, fy, fz, chan = own.shape
    half = fy // 2
    for s in range(2):
        for r in range(2):
            for q in range(2):
                b = 2 * s + r - q
                for a in range(3):
                    place = (a, s, pl.ds(r * 3 * chan, 3 * chan), pl.ds(q * chan, chan))
                    if 0 <= b <= 2:
                        weights[place] = kernel[3 * a + b]
                    else:
                        weights[place] = jnp.zeros((3 * chan, chan), BF16)
    done = 0
    for p in range(planes):
        while done < min(p + 2, planes):
            fill_wide6(wide6, done, lambda y: own[done, y : y + 1].astype(F32))
            done += 1
        pre = None
        for a in range(3):
            if 0 <= p + a - 1 < planes:
                pre = plus(pre, fine_conv(wide6, p + a - 1, weights, a))
        if p == 0:
            edge[0] = pre
        elif p == planes - 1:
            edge[1] = pre
        else:
            act[p - 1], slope[p - 1] = fine_finish(pre, half, fz)


def fine_outer(
    place, from_pair, from_next, weights, edge, act, halo6, pooled, slope, to_pair, to_next, sums
):
    half, fz = act.shape[1:3]
    coarse = pooled.shape[0]
    ends = []
    for e in range(2):
        fill_wide6(
            halo6,
            e,
            lambda y: facing(place, e, from_pair[0, y : y + 1], from_next[0, y : y + 1]),
        )
        total, slope[e] = fine_finish(edge[e] + fine_conv(halo6, e, weights, 2 * e), half, fz)
        if coarse == 1:
            ends.append(total)
            continue
        sums[e] = total + act[0 if e == 0 else 2 * coarse - 3]
    if coarse == 1:
        sums[0] = ends[0] + ends[1]
    for pair in range(1, coarse - 1):
        sums[1 + pair] = act[2 * pair - 1] + act[2 * pair]
    for pair in range(coarse):
        at = 0 if pair == 0 else (1 if pair == coarse - 1 else 1 + pair)
        even = sums[at, :, pl.ds(0, fz // 2, stride=2), :]
        odd = sums[at, :, pl.ds(1, fz // 2, stride=2), :]
        pooled[pair] = ((even + odd) * 0.125).astype(BF16)
    send_planes(place, pooled[0], pooled[coarse - 1], to_pair, to_next)


def coarse_inner(own, kernel, wide3, pre):
    planes, cy, cz, chan = own.shape
    for p in range(planes):
        fill_wide3(wide3, p, own[p].astype(F32))
    for p in range(planes):
        total = None
        for a in range(3):
            if 0 <= p + a - 1 < planes:
                for b in range(3):
                    rows = wide3[p + a - 1, b : b + cy].reshape(cy * cz, 3 * chan)
                    total = plus(total, dot(rows, kernel[3 * a + b]))
        pre[p] = total


def coarse_outer(
    place, from_pair, from_next, kernel, pre, cotangent, halo3, out, delta, to_pair, to_next
):
    planes, cy, cz, wide = cotangent.shape
    for e in range(2):
        fill_wide3(halo3, e, facing(place, e, from_pair[0], from_next[0]))
    for p in range(planes):
        total = pre[p]
        for e in range(2):
            if p == e * (planes - 1):
                for b in range(3):
                    rows = halo3[e, b : b + cy].reshape(cy * cz, halo3.shape[-1])
                    total = total + dot(rows, kernel[6 * e + b])
        sig = jax.nn.sigmoid(total)
        out[p] = (total * sig).astype(BF16).reshape(cy, cz, wide)
        grad = cotangent[p].reshape(cy * cz, wide).astype(F32) * silu_slope(total, sig)
        delta[p] = grad.astype(BF16).reshape(cy, cz, wide)
    send_planes(place, delta[0], delta[planes - 1], to_pair, to_next)


def source(own, halo, plane):
    if plane < 0:
        return halo, 0
    if plane >= own.shape[0]:
        return halo, 1
    return own, plane


def put_term(term, lane, place, orders, keep, send):
    columns = pl.ds(lane, term.shape[1])
    if send is None:
        keep[:, columns] = term.astype(BF16)
        return
    here = place[0] == 0
    rows = term.shape[0] // (2 * len(orders))
    for at, owner in enumerate(orders):
        low = term[owner * rows : (owner + 1) * rows]
        high = term[(owner + 1) * rows : (owner + 2) * rows]
        keep[at, :, columns] = jnp.where(here, low, high).astype(BF16)
        send[at, :, columns] = jnp.where(here, high, low).astype(BF16)


def coarse_terms(place, wide3, halo3, delta, keep, send=None, *, orders, split):
    planes, cy, cz, wide = delta.shape
    span = wide3.shape[-1]
    for tap in range(9):
        a, b = (tap // 3, tap % 3)
        total = None
        for p in range(planes):
            ref, at = source(wide3, halo3, p + a - 1)
            piece = ref[at, b : b + cy].reshape(cy * cz, span)
            total = plus(total, tap_dot(delta[p].reshape(cy * cz, wide), piece))
        put_term(total, tap * span, place, orders[tap >= split], keep, send)


def backward_taps(wide3, plane, kernel, a, grad):
    cy, cz = (wide3.shape[1] - 2, wide3.shape[2])
    wide = kernel.shape[2]
    for b in range(3):
        for c in range(3):
            rows = wide3[plane, b : b + cy, :, c * wide : (c + 1) * wide]
            term = lax.dot_general(
                rows.reshape(cy * cz, wide),
                kernel[26 - (9 * a + 3 * b + c)],
                (((1,), (1,)), ((), ())),
                preferred_element_type=F32,
            )
            grad = plus(grad, term)
    return grad


def coarse_backward(delta, kernel, partial, wide3):
    planes = delta.shape[0]
    for p in range(planes):
        fill_wide3(wide3, p, delta[p].astype(F32))
    for p in range(planes):
        grad = None
        for a in range(3):
            if 0 <= p + a - 1 < planes:
                grad = backward_taps(wide3, p + a - 1, kernel, a, grad)
        partial[p] = grad


def fine_deltas(
    place, from_pair, from_next, kernel, partial, slope, slope_edge, delta, halo3, spread
):
    planes, rows, chan = partial.shape
    cy, fz = spread.shape[:2]
    cz = fz // 2
    for e in range(2):
        fill_wide3(halo3, e, facing(place, e, from_pair[0], from_next[0]))
    for p in range(planes):
        grad = partial[p]
        for e in range(2):
            if p == e * (planes - 1):
                grad = backward_taps(halo3, e, kernel, 2 * e, grad)
        grad = grad.astype(BF16).astype(F32).reshape(cy, cz, chan) * 0.125
        spread[:, pl.ds(0, cz, stride=2), :] = grad
        spread[:, pl.ds(1, cz, stride=2), :] = grad
        near = spread[...]
        both = jnp.concatenate([near, near], axis=-1)
        for at in range(2 * p, 2 * p + 2):
            ref, index = source(slope, slope_edge, at - 1)
            delta[at] = (both * ref[index].astype(F32)).astype(BF16)


def fine_part(place, wide6, halo6, delta, keep, send, order, taps):
    planes, half, fz, double = delta.shape
    chan = double // 2
    three = 3 * chan
    for tap in taps:
        a, b = (tap // 3, tap % 3)
        total = None
        for p in range(planes):
            ref, at = source(wide6, halo6, p + a - 1)
            for q in range(2):
                pair, parity = ((q + b) // 2, (q + b) % 2)
                rows = delta[p, :, :, q * chan : (q + 1) * chan].reshape(half * fz, chan)
                piece = ref[at, pair : pair + half, :, parity * three : (parity + 1) * three]
                total = plus(total, tap_dot(rows, piece.reshape(half * fz, three)))
        put_term(total, (tap - taps[0]) * three, place, order, keep, send)


def fine_first(
    place, from_pair, from_next, kernel, partial, slope, slope_edge, wide6, halo6, *rest, order, taps
):
    if len(rest) == 5:
        delta, keep, send, halo3, spread = rest
    else:
        delta, keep, halo3, spread = rest
        send = None
    fine_deltas(
        place, from_pair, from_next, kernel, partial, slope, slope_edge, delta, halo3, spread
    )
    fine_part(place, wide6, halo6, delta, keep, send, order, taps)


def fine_second(place, wide6, halo6, delta, keep, send=None, *, order, taps):
    fine_part(place, wide6, halo6, delta, keep, send, order, taps)


def swap(value, bit):
    count = lax.axis_size("space")
    return lax.ppermute(value, "space", [(i, i ^ bit) for i in range(count)])


def swap_sample(value, bit=0):
    count = lax.axis_size("space")
    return lax.ppermute(
        value,
        ("sample", "space"),
        [(s * count + i, (1 - s) * count + (i ^ bit)) for s in range(2) for i in range(count)],
    )


def middle_bits(count):
    bits = [1 << k for k in range(1, count.bit_length() - 2)]
    return bits, bits[1:] + bits[:1]


def order_of(middle, count):
    bits = middle + [count // 2]
    return [
        sum(bit for k, bit in enumerate(bits) if at >> (len(bits) - 1 - k) & 1)
        for at in range(count // 2)
    ]


def term_shapes(rows, columns, count):
    owned = rows // count
    if owned % 8:
        return [jax.ShapeDtypeStruct((rows, columns), BF16)]
    return [jax.ShapeDtypeStruct((count // 2, owned, columns), BF16)] * 2


def pick(parts, bit):
    mine = lax.axis_index("space") // bit % 2
    keep = lax.dynamic_index_in_dim(parts, mine, 0, keepdims=False)
    return keep, lax.dynamic_index_in_dim(parts, 1 - mine, 0, keepdims=False)


def sided(terms, middle, count, columns):
    if len(terms) == 2:
        return [item[:, :, columns] for item in terms]
    whole = terms[0][:, columns]
    bits = count.bit_length() - 1
    parts = whole.reshape((2,) * bits + (whole.shape[0] // count, -1))
    sequence = [1] + middle + [count // 2]
    axes = [bits - bit.bit_length() for bit in sequence]
    return pick(parts.transpose(tuple(axes) + (bits, bits + 1)), 1)


def halved(total, middle):
    for bit in middle:
        owned, columns = total.shape[-2:]
        keep, send = pick(total.reshape(2, -1, owned, columns), bit)
        total = keep + swap(send.astype(BF16), bit).astype(F32)
    return total.reshape((2,) + total.shape[-2:])


def last_halved(total):
    bit = lax.axis_size("space") // 2
    keep, send = pick(total, bit)
    base = (keep + swap(send.astype(BF16), bit).astype(F32)).astype(BF16)
    if lax.axis_size("sample") != 2:
        return lax.psum(base, "sample").astype(F32)
    return base.astype(F32) + swap_sample(base).astype(F32)


def last_direct(total):
    if lax.axis_size("sample") != 2:
        return last_halved(total)
    bit = lax.axis_size("space") // 2
    keep, send = pick(total.astype(BF16), bit)
    near, cross, other = (swap(send, bit), swap_sample(send, bit), swap_sample(keep))
    return (keep.astype(F32) + other.astype(F32)) + (near.astype(F32) + cross.astype(F32))


def shards(volumes, fine_kernel, coarse_kernel, cotangent):
    planes, fy, fz, chan = volumes.shape[1:]
    wide = coarse_kernel.shape[2]
    cp, cy, cz = (planes // 2, fy // 2, fz // 2)
    half = fy // 2
    count = lax.axis_size("space")
    me = lax.axis_index("space")
    parity = me % 2
    place = jnp.reshape(parity, (1,)).astype(jnp.int32)
    x = volumes[0]
    cells, few = (planes * fy * fz, cp * cy * cz)
    fine_flops, coarse_flops = (54 * cells * chan * chan, 54 * few * chan * wide)

    def shape(*extents, kind=BF16):
        return jax.ShapeDtypeStruct(extents, kind)

    to_pair = lax.dynamic_slice_in_dim(x, (1 - parity) * (planes - 1), 1, axis=0)
    to_next = lax.dynamic_slice_in_dim(x, parity * (planes - 1), 1, axis=0)
    from_pair, from_next = exchange(to_pair, to_next)
    mid = max(planes - 2, 1)
    wide6, weights, edge, act, slope = kernel_call(
        fine_inner,
        [x, fine_kernel.reshape(9, 3 * chan, chan)],
        [
            shape(planes, half + 1, fz, 6 * chan),
            shape(3, 2, 6 * chan, 2 * chan),
            shape(2, half * fz, 2 * chan, kind=F32),
            shape(mid, half, fz, chan, kind=F32),
            shape(mid, half, fz, 2 * chan),
        ],
        [],
        fine_flops,
        16,
    )
    halo6, pooled, slope_edge, to_pair, to_next = kernel_call(
        fine_outer,
        [place, from_pair, from_next, weights, edge, act],
        [
            shape(2, half + 1, fz, 6 * chan),
            shape(cp, cy, cz, chan),
            shape(2, half, fz, 2 * chan),
            shape(1, cy, cz, chan),
            shape(1, cy, cz, chan),
        ],
        [pltpu.VMEM((max(cp, 2), half, fz, chan), F32)],
        fine_flops // 6,
        16,
        scalars=1,
    )
    from_pair, from_next = exchange(to_pair, to_next)
    taps = coarse_kernel.reshape(9, 3 * chan, wide)
    wide3, pre = kernel_call(
        coarse_inner,
        [pooled, taps],
        [shape(cp, cy + 2, cz, 3 * chan), shape(cp, cy * cz, wide, kind=F32)],
        [],
        coarse_flops,
        16,
    )
    halo3, out, coarse_delta, to_pair, to_next = kernel_call(
        coarse_outer,
        [place, from_pair, from_next, taps, pre, cotangent[0]],
        [
            shape(2, cy + 2, cz, 3 * chan),
            shape(cp, cy, cz, wide),
            shape(cp, cy, cz, wide),
            shape(1, cy, cz, wide),
            shape(1, cy, cz, wide),
        ],
        [],
        coarse_flops // 3,
        16,
        scalars=1,
    )
    from_pair, from_next = exchange(to_pair, to_next)
    first, second = middle_bits(count)
    orders = (order_of(first, count), order_of(second, count))
    split = 5
    border = split * 3 * chan
    low, high = (slice(0, border), slice(border, 27 * chan))
    terms = kernel_call(
        functools.partial(coarse_terms, orders=orders, split=split),
        [place, wide3, halo3, coarse_delta],
        term_shapes(wide, 27 * chan, count),
        [],
        coarse_flops,
        16,
        scalars=1,
    )
    halves = [sided(terms, first, count, low), sided(terms, second, count, high)]
    if len(terms) == 2:
        got = swap(terms[1], 1)
        gots = [got[:, :, low], got[:, :, high]]
    else:
        gots = [swap(send, 1) for keep, send in halves]
    sums = []
    for (keep, _), got, middle in zip(halves, gots, (first, second)):
        sums.append(halved(keep.astype(F32) + got.astype(F32), middle))
    coarse_grad = last_halved(jnp.concatenate(sums, axis=-1))

    (partial,) = kernel_call(
        coarse_backward,
        [coarse_delta, coarse_kernel],
        [shape(cp, cy * cz, chan, kind=F32)],
        [pltpu.VMEM((cp, cy + 2, cz, 3 * wide), BF16)],
        coarse_flops,
        16,
        after=[terms[-1]],
    )
    fine_delta, *one = kernel_call(
        functools.partial(fine_first, order=orders[0], taps=range(split)),
        [place, from_pair, from_next, coarse_kernel, partial, slope, slope_edge, wide6, halo6],
        [shape(planes, half, fz, 2 * chan)] + term_shapes(chan, border, count),
        [pltpu.VMEM((2, cy + 2, cz, 3 * wide), BF16), pltpu.VMEM((cy, fz, chan), F32)],
        fine_flops * 2 // 3,
        16,
        scalars=1,
    )
    two = kernel_call(
        functools.partial(fine_second, order=orders[1], taps=range(split, 9)),
        [place, wide6, halo6, fine_delta],
        term_shapes(chan, 27 * chan - border, count),
        [],
        fine_flops // 2,
        16,
        scalars=1,
    )
    sums = []
    for terms, middle in ((one, first), (two, second)):
        keep, send = sided(terms, middle, count, slice(None))
        sums.append(halved(keep.astype(F32) + swap(send, 1).astype(F32), middle))
    fine_grad = last_direct(jnp.concatenate(sums, axis=-1))
    return (out[None], fine_grad, coarse_grad)


def solution(mesh):
    placed = (
        P("sample", "space", None, None, None),
        P(),
        P(),
        P("sample", "space", None, None, None),
    )
    return jax.shard_map(
        shards,
        mesh=mesh,
        in_specs=placed,
        out_specs=(P("sample", "space", None, None, None), P("space", None), P("space", None)),
        check_vma=False,
    )
```

```python
import functools

import jax
import jax.numpy as jnp
from jax import lax
from jax.experimental import pallas as pl
from jax.experimental.pallas import tpu as pltpu
from jax.sharding import PartitionSpec as P

F32 = jnp.float32
BF16 = jnp.bfloat16
COST = 64
VMEM = pl.BlockSpec(memory_space=pltpu.VMEM)
SMEM = pl.BlockSpec(memory_space=pltpu.SMEM)


def kernel_call(body, operands, outs, scratch, flops, limit, scalars=0, after=()):
    cost = pl.CostEstimate(flops=flops // COST, bytes_accessed=2**20, transcendentals=0)
    used, extra = (len(operands), len(after))
    specs = [SMEM] * scalars + [VMEM] * (used - scalars + extra)

    def inner(*refs):
        body(*refs[:used], *refs[used + extra :])

    return pl.pallas_call(
        inner,
        out_shape=outs,
        in_specs=specs,
        out_specs=[VMEM] * len(outs),
        scratch_shapes=scratch,
        cost_estimate=cost,
        compiler_params=pltpu.CompilerParams(vmem_limit_bytes=limit * 2**20),
    )(*operands, *after)


def exchange(to_pair, to_next):
    count = lax.axis_size("space")
    pair = [(i, i ^ 1) for i in range(count) if i ^ 1 < count]
    odd = [i for i in range(1, count - 1, 2)]
    across = [(i, i + 1) for i in odd] + [(i + 1, i) for i in odd]
    return lax.ppermute(to_pair, "space", pair), lax.ppermute(to_next, "space", across)


def silu_slope(value, sig):
    return sig * (1.0 + value * (1.0 - sig))


def three_shifts(value):
    depth = value.shape[1]
    at = lax.broadcasted_iota(jnp.int32, value.shape, 1)
    lower = jnp.where(at == 0, 0.0, pltpu.roll(value, 1, 1))
    upper = jnp.where(at == depth - 1, 0.0, pltpu.roll(value, depth - 1, 1))
    return lower, value, upper


def facing(place, edge, from_pair, from_next):
    return jnp.where(place[0] != edge, from_pair.astype(F32), from_next.astype(F32))


def send_planes(place, first, last, to_pair, to_next):
    even = place[0] == 0
    first, last = (first.astype(F32), last.astype(F32))
    to_pair[0] = jnp.where(even, last, first).astype(BF16)
    to_next[0] = jnp.where(even, first, last).astype(BF16)


def dot(left, right):
    return jnp.dot(left, right, preferred_element_type=F32)


def tap_dot(left, right):
    return lax.dot_general(left, right, (((0,), (0,)), ((), ())), preferred_element_type=F32)


def plus(total, term):
    return term if total is None else total + term


def fill_wide6(target, plane, row_of):
    half = target.shape[1] - 1
    depth, lanes = target.shape[2:]
    three = lanes // 2
    zero = jnp.zeros((depth, three), BF16)
    target[plane, 0, :, 0:three] = zero
    target[plane, half, :, three:lanes] = zero
    for y in range(2 * half):
        pair, parity = ((y + 1) // 2, (y + 1) % 2)
        for c, piece in enumerate(three_shifts(row_of(y))):
            lane = parity * three + c * (three // 3)
            target[plane, pair : pair + 1, :, lane : lane + three // 3] = piece.astype(BF16)


def fill_wide3(target, plane, value):
    rows, depth, chan = value.shape
    zero = jnp.zeros((depth, 3 * chan), BF16)
    target[plane, 0] = zero
    target[plane, rows + 1] = zero
    for c, piece in enumerate(three_shifts(value)):
        target[plane, 1 : rows + 1, :, c * chan : (c + 1) * chan] = piece.astype(BF16)


def fine_conv(wide6, plane, weights, a):
    half = wide6.shape[1] - 1
    total = None
    for s in range(2):
        rows = wide6[plane, s : s + half].reshape(half * wide6.shape[2], wide6.shape[3])
        total = plus(total, dot(rows, weights[a, s]))
    return total


def fine_finish(pre, half, depth):
    chan = pre.shape[1] // 2
    sig = jax.nn.sigmoid(pre)
    act = (pre * sig).astype(BF16).astype(F32)
    slope = silu_slope(pre, sig).astype(BF16).reshape(half, depth, 2 * chan)
    return (act[:, :chan] + act[:, chan:]).reshape(half, depth, chan), slope


def fine_inner(own, kernel, wide6, weights, edge, act, slope):
    planes, fy, fz, chan = own.shape
    half = fy // 2
    for s in range(2):
        for r in range(2):
            for q in range(2):
                b = 2 * s + r - q
                for a in range(3):
                    place = (a, s, pl.ds(r * 3 * chan, 3 * chan), pl.ds(q * chan, chan))
                    if 0 <= b <= 2:
                        weights[place] = kernel[3 * a + b]
                    else:
                        weights[place] = jnp.zeros((3 * chan, chan), BF16)
    done = 0
    for p in range(planes):
        while done < min(p + 2, planes):
            fill_wide6(wide6, done, lambda y: own[done, y : y + 1].astype(F32))
            done += 1
        pre = None
        for a in range(3):
            if 0 <= p + a - 1 < planes:
                pre = plus(pre, fine_conv(wide6, p + a - 1, weights, a))
        if p == 0:
            edge[0] = pre
        elif p == planes - 1:
            edge[1] = pre
        else:
            act[p - 1], slope[p - 1] = fine_finish(pre, half, fz)


def fine_outer(
    place, from_pair, from_next, weights, edge, act, halo6, pooled, slope, to_pair, to_next, sums
):
    half, fz = act.shape[1:3]
    coarse = pooled.shape[0]
    ends = []
    for e in range(2):
        fill_wide6(
            halo6,
            e,
            lambda y: facing(place, e, from_pair[0, y : y + 1], from_next[0, y : y + 1]),
        )
        total, slope[e] = fine_finish(edge[e] + fine_conv(halo6, e, weights, 2 * e), half, fz)
        if coarse == 1:
            ends.append(total)
            continue
        sums[e] = total + act[0 if e == 0 else 2 * coarse - 3]
    if coarse == 1:
        sums[0] = ends[0] + ends[1]
    for pair in range(1, coarse - 1):
        sums[1 + pair] = act[2 * pair - 1] + act[2 * pair]
    for pair in range(coarse):
        at = 0 if pair == 0 else (1 if pair == coarse - 1 else 1 + pair)
        even = sums[at, :, pl.ds(0, fz // 2, stride=2), :]
        odd = sums[at, :, pl.ds(1, fz // 2, stride=2), :]
        pooled[pair] = ((even + odd) * 0.125).astype(BF16)
    send_planes(place, pooled[0], pooled[coarse - 1], to_pair, to_next)


def coarse_inner(own, kernel, wide3, pre):
    planes, cy, cz, chan = own.shape
    for p in range(planes):
        fill_wide3(wide3, p, own[p].astype(F32))
    for p in range(planes):
        total = None
        for a in range(3):
            if 0 <= p + a - 1 < planes:
                for b in range(3):
                    rows = wide3[p + a - 1, b : b + cy].reshape(cy * cz, 3 * chan)
                    total = plus(total, dot(rows, kernel[3 * a + b]))
        pre[p] = total


def coarse_outer(
    place, from_pair, from_next, kernel, pre, cotangent, halo3, out, delta, to_pair, to_next
):
    planes, cy, cz, wide = cotangent.shape
    for e in range(2):
        fill_wide3(halo3, e, facing(place, e, from_pair[0], from_next[0]))
    for p in range(planes):
        total = pre[p]
        for e in range(2):
            if p == e * (planes - 1):
                for b in range(3):
                    rows = halo3[e, b : b + cy].reshape(cy * cz, halo3.shape[-1])
                    total = total + dot(rows, kernel[6 * e + b])
        sig = jax.nn.sigmoid(total)
        out[p] = (total * sig).astype(BF16).reshape(cy, cz, wide)
        grad = cotangent[p].reshape(cy * cz, wide).astype(F32) * silu_slope(total, sig)
        delta[p] = grad.astype(BF16).reshape(cy, cz, wide)
    send_planes(place, delta[0], delta[planes - 1], to_pair, to_next)


def source(own, halo, plane):
    if plane < 0:
        return halo, 0
    if plane >= own.shape[0]:
        return halo, 1
    return own, plane


def put_term(term, lane, place, orders, keep, send):
    columns = pl.ds(lane, term.shape[1])
    if send is None:
        keep[:, columns] = term.astype(BF16)
        return
    here = place[0] == 0
    rows = term.shape[0] // (2 * len(orders))
    for at, owner in enumerate(orders):
        low = term[owner * rows : (owner + 1) * rows]
        high = term[(owner + 1) * rows : (owner + 2) * rows]
        keep[at, :, columns] = jnp.where(here, low, high).astype(BF16)
        send[at, :, columns] = jnp.where(here, high, low).astype(BF16)


def coarse_terms(place, wide3, halo3, delta, keep, send=None, *, order):
    planes, cy, cz, wide = delta.shape
    span = wide3.shape[-1]
    for tap in range(9):
        a, b = (tap // 3, tap % 3)
        total = None
        for p in range(planes):
            ref, at = source(wide3, halo3, p + a - 1)
            piece = ref[at, b : b + cy].reshape(cy * cz, span)
            total = plus(total, tap_dot(delta[p].reshape(cy * cz, wide), piece))
        put_term(total, tap * span, place, order, keep, send)


def backward_taps(wide3, plane, kernel, a, grad):
    cy, cz = (wide3.shape[1] - 2, wide3.shape[2])
    wide = kernel.shape[2]
    for b in range(3):
        for c in range(3):
            rows = wide3[plane, b : b + cy, :, c * wide : (c + 1) * wide]
            term = lax.dot_general(
                rows.reshape(cy * cz, wide),
                kernel[26 - (9 * a + 3 * b + c)],
                (((1,), (1,)), ((), ())),
                preferred_element_type=F32,
            )
            grad = plus(grad, term)
    return grad


def coarse_backward(delta, kernel, partial, wide3):
    planes = delta.shape[0]
    for p in range(planes):
        fill_wide3(wide3, p, delta[p].astype(F32))
    for p in range(planes):
        grad = None
        for a in range(3):
            if 0 <= p + a - 1 < planes:
                grad = backward_taps(wide3, p + a - 1, kernel, a, grad)
        partial[p] = grad


def fine_deltas(
    place, from_pair, from_next, kernel, partial, slope, slope_edge, delta, halo3, spread
):
    planes, rows, chan = partial.shape
    cy, fz = spread.shape[:2]
    cz = fz // 2
    for e in range(2):
        fill_wide3(halo3, e, facing(place, e, from_pair[0], from_next[0]))
    for p in range(planes):
        grad = partial[p]
        for e in range(2):
            if p == e * (planes - 1):
                grad = backward_taps(halo3, e, kernel, 2 * e, grad)
        grad = grad.astype(BF16).astype(F32).reshape(cy, cz, chan) * 0.125
        spread[:, pl.ds(0, cz, stride=2), :] = grad
        spread[:, pl.ds(1, cz, stride=2), :] = grad
        near = spread[...]
        both = jnp.concatenate([near, near], axis=-1)
        for at in range(2 * p, 2 * p + 2):
            ref, index = source(slope, slope_edge, at - 1)
            delta[at] = (both * ref[index].astype(F32)).astype(BF16)


def fine_part(place, wide6, halo6, delta, keep, send, order, taps):
    planes, half, fz, double = delta.shape
    chan = double // 2
    three = 3 * chan
    for tap in taps:
        a, b = (tap // 3, tap % 3)
        total = None
        for p in range(planes):
            ref, at = source(wide6, halo6, p + a - 1)
            for q in range(2):
                pair, parity = ((q + b) // 2, (q + b) % 2)
                rows = delta[p, :, :, q * chan : (q + 1) * chan].reshape(half * fz, chan)
                piece = ref[at, pair : pair + half, :, parity * three : (parity + 1) * three]
                total = plus(total, tap_dot(rows, piece.reshape(half * fz, three)))
        put_term(total, (tap - taps[0]) * three, place, order, keep, send)


def fine_first(
    place, from_pair, from_next, kernel, partial, slope, slope_edge, wide6, halo6, *rest, order, taps
):
    if len(rest) == 5:
        delta, keep, send, halo3, spread = rest
    else:
        delta, keep, halo3, spread = rest
        send = None
    fine_deltas(
        place, from_pair, from_next, kernel, partial, slope, slope_edge, delta, halo3, spread
    )
    fine_part(place, wide6, halo6, delta, keep, send, order, taps)


def fine_second(place, wide6, halo6, delta, keep, send=None, *, order, taps):
    fine_part(place, wide6, halo6, delta, keep, send, order, taps)


def swap(value, bit):
    count = lax.axis_size("space")
    return lax.ppermute(value, "space", [(i, i ^ bit) for i in range(count)])


def swap_sample(value, bit=0):
    count = lax.axis_size("space")
    return lax.ppermute(
        value,
        ("sample", "space"),
        [(s * count + i, (1 - s) * count + (i ^ bit)) for s in range(2) for i in range(count)],
    )


def exchange_groups(count):
    bits = [1 << k for k in range(1, count.bit_length() - 2)]
    return [bits[k : k + 2] for k in range(0, len(bits), 2)]


def exchange_bits(count):
    return [bit for group in exchange_groups(count) for bit in group] + [count // 2]


def owners_in_order(count):
    bits = exchange_bits(count)
    return [
        sum(bit for k, bit in enumerate(bits) if at >> (len(bits) - 1 - k) & 1)
        for at in range(count // 2)
    ]


def term_shapes(rows, columns, count):
    owned = rows // count
    if owned % 8:
        return [jax.ShapeDtypeStruct((rows, columns), BF16)]
    return [jax.ShapeDtypeStruct((count // 2, owned, columns), BF16)] * 2


def pick(parts, bit):
    mine = lax.axis_index("space") // bit % 2
    keep = lax.dynamic_index_in_dim(parts, mine, 0, keepdims=False)
    return keep, lax.dynamic_index_in_dim(parts, 1 - mine, 0, keepdims=False)


def sided(terms, count):
    if len(terms) == 2:
        return terms
    bits = count.bit_length() - 1
    parts = terms[0].reshape((2,) * bits + (terms[0].shape[0] // count, -1))
    axes = [bits - bit.bit_length() for bit in [1] + exchange_bits(count)]
    sides = pick(parts.transpose(tuple(axes) + (bits, bits + 1)), 1)
    return [side.reshape((-1,) + side.shape[-2:]) for side in sides]


def masks_of(group):
    return [sum(bit for k, bit in enumerate(group) if turn >> k & 1) for turn in range(1 << len(group))]


def fold_body(place, *refs, group, chunks):
    pieces, outs = (refs[: sum(chunks)], refs[sum(chunks) :])
    span = outs[0].shape[0]
    lane = start = 0
    for length in chunks:
        some = pieces[start : start + length]
        columns = pl.ds(lane, some[0].shape[2])
        for mask, out in zip(masks_of(group), outs):
            at = 0
            for bit in group:
                mine = place[bit.bit_length() - 1]
                at = 2 * at + (1 - mine if mask & bit else mine)
            for k in range(span):
                total = None
                for piece in some:
                    total = plus(total, piece[at * span + k].astype(F32))
                out[k, :, columns] = total.astype(out.dtype)
        start += length
        lane += some[0].shape[2]


def fold(place, chunks, group, after=()):
    length, owned = chunks[0][0].shape[:2]
    extents = (length >> len(group), owned, sum(some[0].shape[2] for some in chunks))
    masks = masks_of(group)
    kept, *sends = kernel_call(
        functools.partial(fold_body, group=group, chunks=[len(some) for some in chunks]),
        [place] + [piece for some in chunks for piece in some],
        [jax.ShapeDtypeStruct(extents, BF16 if mask else F32) for mask in masks],
        [],
        0,
        8,
        scalars=1,
        after=after,
    )
    return dict(zip(masks[1:], sends)), kept


def received(sends, kept):
    return [kept] + [swap(part, mask) for mask, part in sends.items()]


def last_sum(sends, kept):
    bit = lax.axis_size("space") // 2
    base = (kept[0] + swap(sends[bit][0], bit).astype(F32)).astype(BF16)
    if lax.axis_size("sample") != 2:
        return lax.psum(base, "sample").astype(F32)
    return base.astype(F32) + swap_sample(base).astype(F32)


def last_direct(sends, kept):
    if lax.axis_size("sample") != 2:
        return last_sum(sends, kept)
    bit = lax.axis_size("space") // 2
    keep, send = (kept[0].astype(BF16), sends[bit][0])
    near, cross, other = (swap(send, bit), swap_sample(send, bit), swap_sample(keep))
    return (keep.astype(F32) + other.astype(F32)) + (near.astype(F32) + cross.astype(F32))


def shards(volumes, fine_kernel, coarse_kernel, cotangent):
    planes, fy, fz, chan = volumes.shape[1:]
    wide = coarse_kernel.shape[2]
    cp, cy, cz = (planes // 2, fy // 2, fz // 2)
    half = fy // 2
    count = lax.axis_size("space")
    me = lax.axis_index("space")
    parity = me % 2
    place = jnp.stack([me >> k & 1 for k in range(count.bit_length() - 1)]).astype(jnp.int32)
    x = volumes[0]
    cells, few = (planes * fy * fz, cp * cy * cz)
    fine_flops, coarse_flops = (54 * cells * chan * chan, 54 * few * chan * wide)

    def shape(*extents, kind=BF16):
        return jax.ShapeDtypeStruct(extents, kind)

    to_pair = lax.dynamic_slice_in_dim(x, (1 - parity) * (planes - 1), 1, axis=0)
    to_next = lax.dynamic_slice_in_dim(x, parity * (planes - 1), 1, axis=0)
    from_pair, from_next = exchange(to_pair, to_next)
    mid = max(planes - 2, 1)
    wide6, weights, edge, act, slope = kernel_call(
        fine_inner,
        [x, fine_kernel.reshape(9, 3 * chan, chan)],
        [
            shape(planes, half + 1, fz, 6 * chan),
            shape(3, 2, 6 * chan, 2 * chan),
            shape(2, half * fz, 2 * chan, kind=F32),
            shape(mid, half, fz, chan, kind=F32),
            shape(mid, half, fz, 2 * chan),
        ],
        [],
        fine_flops,
        16,
    )
    halo6, pooled, slope_edge, to_pair, to_next = kernel_call(
        fine_outer,
        [place, from_pair, from_next, weights, edge, act],
        [
            shape(2, half + 1, fz, 6 * chan),
            shape(cp, cy, cz, chan),
            shape(2, half, fz, 2 * chan),
            shape(1, cy, cz, chan),
            shape(1, cy, cz, chan),
        ],
        [pltpu.VMEM((max(cp, 2), half, fz, chan), F32)],
        fine_flops // 6,
        16,
        scalars=1,
    )
    from_pair, from_next = exchange(to_pair, to_next)
    taps = coarse_kernel.reshape(9, 3 * chan, wide)
    wide3, pre = kernel_call(
        coarse_inner,
        [pooled, taps],
        [shape(cp, cy + 2, cz, 3 * chan), shape(cp, cy * cz, wide, kind=F32)],
        [],
        coarse_flops,
        16,
    )
    halo3, out, coarse_delta, to_pair, to_next = kernel_call(
        coarse_outer,
        [place, from_pair, from_next, taps, pre, cotangent[0]],
        [
            shape(2, cy + 2, cz, 3 * chan),
            shape(cp, cy, cz, wide),
            shape(cp, cy, cz, wide),
            shape(1, cy, cz, wide),
            shape(1, cy, cz, wide),
        ],
        [],
        coarse_flops // 3,
        16,
        scalars=1,
    )
    from_pair, from_next = exchange(to_pair, to_next)
    order = owners_in_order(count)
    steps = exchange_groups(count) + [[count // 2]]
    terms = kernel_call(
        functools.partial(coarse_terms, order=order),
        [place, wide3, halo3, coarse_delta],
        term_shapes(wide, 27 * chan, count),
        [],
        coarse_flops,
        16,
        scalars=1,
    )
    keep, send = sided(terms, count)
    early, coarse_kept = fold(
        place, [[keep, swap(send, 1)]], steps[0], [from_pair, from_next]
    )
    (partial,) = kernel_call(
        coarse_backward,
        [coarse_delta, coarse_kernel],
        [shape(cp, cy * cz, chan, kind=F32)],
        [pltpu.VMEM((cp, cy + 2, cz, 3 * wide), BF16)],
        coarse_flops,
        16,
        after=[terms[-1]],
    )
    parts = [range(0, 3), range(3, 6), range(6, 9)]
    fine_delta, *first = kernel_call(
        functools.partial(fine_first, order=order, taps=parts[0]),
        [place, from_pair, from_next, coarse_kernel, partial, slope, slope_edge, wide6, halo6],
        [shape(planes, half, fz, 2 * chan)] + term_shapes(chan, 9 * chan, count),
        [pltpu.VMEM((2, cy + 2, cz, 3 * wide), BF16), pltpu.VMEM((cy, fz, chan), F32)],
        fine_flops * 2 // 3,
        16,
        scalars=1,
        after=list(early.values())[:1],
    )
    fine_parts = [first]
    for part in parts[1:]:
        fine_parts.append(
            kernel_call(
                functools.partial(fine_second, order=order, taps=part),
                [place, wide6, halo6, fine_delta],
                term_shapes(chan, 9 * chan, count),
                [],
                fine_flops // 3,
                16,
                scalars=1,
                after=[fine_parts[-1][-1]],
            )
        )
    got = received(early, coarse_kept)
    pieces = []
    for part in fine_parts:
        keep, send = sided(part, count)
        pieces.append([keep, swap(send, 1)])
    late, fine_kept = fold(place, pieces, steps[0], got[1:])
    for group in steps[1:]:
        early, coarse_kept = fold(place, [got], group, [late[steps[0][0]]])
        got = received(early, coarse_kept)
    coarse_grad = last_sum(early, coarse_kept)
    for group in steps[1:]:
        late, fine_kept = fold(place, [received(late, fine_kept)], group)
    fine_grad = last_direct(late, fine_kept)
    return (out[None], fine_grad, coarse_grad)


def solution(mesh):
    placed = (
        P("sample", "space", None, None, None),
        P(),
        P(),
        P("sample", "space", None, None, None),
    )
    return jax.shard_map(
        shards,
        mesh=mesh,
        in_specs=placed,
        out_specs=(P("sample", "space", None, None, None), P("space", None), P("space", None)),
        check_vma=False,
    )
```

```python
import functools

import jax
import jax.numpy as jnp
from jax import lax
from jax.experimental import pallas as pl
from jax.experimental.pallas import tpu as pltpu
from jax.sharding import PartitionSpec as P

F32 = jnp.float32
BF16 = jnp.bfloat16
COST = 64
FETCH = 60
PARTS = (range(0, 2), range(2, 6), range(6, 9))
VMEM = pl.BlockSpec(memory_space=pltpu.VMEM)
SMEM = pl.BlockSpec(memory_space=pltpu.SMEM)


def kernel_call(body, operands, outs, scratch, flops, limit, scalars=0, after=()):
    cost = pl.CostEstimate(flops=flops // COST, bytes_accessed=2**20, transcendentals=0)
    used, extra = (len(operands), len(after))
    specs = [SMEM] * scalars + [VMEM] * (used - scalars + extra)

    def inner(*refs):
        body(*refs[:used], *refs[used + extra :])

    return pl.pallas_call(
        inner,
        out_shape=outs,
        in_specs=specs,
        out_specs=[VMEM] * len(outs),
        scratch_shapes=scratch,
        cost_estimate=cost,
        compiler_params=pltpu.CompilerParams(vmem_limit_bytes=limit * 2**20),
    )(*operands, *after)


def exchange(to_pair, to_next):
    count = lax.axis_size("space")
    pair = [(i, i ^ 1) for i in range(count) if i ^ 1 < count]
    odd = [i for i in range(1, count - 1, 2)]
    across = [(i, i + 1) for i in odd] + [(i + 1, i) for i in odd]
    return lax.ppermute(to_pair, "space", pair), lax.ppermute(to_next, "space", across)


def silu_slope(value, sig):
    return sig * (1.0 + value * (1.0 - sig))


def three_shifts(value):
    depth = value.shape[1]
    at = lax.broadcasted_iota(jnp.int32, value.shape, 1)
    lower = jnp.where(at == 0, 0.0, pltpu.roll(value, 1, 1))
    upper = jnp.where(at == depth - 1, 0.0, pltpu.roll(value, depth - 1, 1))
    return lower, value, upper


def facing(place, edge, from_pair, from_next):
    return jnp.where(place[0] % 2 != edge, from_pair.astype(F32), from_next.astype(F32))


def dot(left, right):
    return jnp.dot(left, right, preferred_element_type=F32)


def tap_dot(left, right):
    return lax.dot_general(left, right, (((0,), (0,)), ((), ())), preferred_element_type=F32)


def plus(total, term):
    return term if total is None else total + term


def fill_wide6(target, plane, row_of):
    half = target.shape[1] - 1
    depth, lanes = target.shape[2:]
    three = lanes // 2
    zero = jnp.zeros((depth, three), BF16)
    target[plane, 0, :, 0:three] = zero
    target[plane, half, :, three:lanes] = zero
    for y in range(2 * half):
        pair, parity = ((y + 1) // 2, (y + 1) % 2)
        for c, piece in enumerate(three_shifts(row_of(y))):
            lane = parity * three + c * (three // 3)
            target[plane, pair : pair + 1, :, lane : lane + three // 3] = piece.astype(BF16)


def fill_wide3(target, plane, value):
    rows, depth, chan = value.shape
    zero = jnp.zeros((depth, 3 * chan), BF16)
    target[plane, 0] = zero
    target[plane, rows + 1] = zero
    for c, piece in enumerate(three_shifts(value)):
        target[plane, 1 : rows + 1, :, c * chan : (c + 1) * chan] = piece.astype(BF16)


def fine_conv(wide6, plane, weights, a):
    half = wide6.shape[1] - 1
    total = None
    for s in range(2):
        rows = wide6[plane, s : s + half].reshape(half * wide6.shape[2], wide6.shape[3])
        total = plus(total, dot(rows, weights[a, s]))
    return total


def fine_finish(pre, half, depth):
    chan = pre.shape[1] // 2
    sig = jax.nn.sigmoid(pre)
    act = (pre * sig).astype(BF16).astype(F32)
    slope = silu_slope(pre, sig).astype(BF16).reshape(half, depth, 2 * chan)
    return (act[:, :chan] + act[:, chan:]).reshape(half, depth, chan), slope


def side_planes(place, volume, cotangent, to_pair, to_next, sems):
    planes, rows, _, chan = volume.shape
    cp, cy = cotangent.shape[:2]
    copies = []
    for to, side in ((to_pair, 1 - place[0] % 2), (to_next, place[0] % 2)):
        copies.append((volume.at[side * (planes - 1)], to.at[pl.ds(0, rows)]))
        for k in range(cotangent.shape[3] // chan):
            part = cotangent.at[side * (cp - 1), :, :, pl.ds(k * chan, chan)]
            copies.append((part, to.at[pl.ds(rows + k * cy, cy)]))
    copies = [pltpu.make_async_copy(*pair, sems.at[k]) for k, pair in enumerate(copies)]
    for copy in copies:
        copy.start()
    for copy in copies:
        copy.wait()


def fine_inner(own, kernel, wide6, weights, edge, act, slope):
    planes, fy, fz, chan = own.shape
    half = fy // 2
    for s in range(2):
        for r in range(2):
            for q in range(2):
                b = 2 * s + r - q
                for a in range(3):
                    place = (a, s, pl.ds(r * 3 * chan, 3 * chan), pl.ds(q * chan, chan))
                    if 0 <= b <= 2:
                        weights[place] = kernel[3 * a + b]
                    else:
                        weights[place] = jnp.zeros((3 * chan, chan), BF16)
    done = 0
    for p in range(planes):
        while done < min(p + 2, planes):
            fill_wide6(wide6, done, lambda y: own[done, y : y + 1].astype(F32))
            done += 1
        pre = None
        for a in range(3):
            if 0 <= p + a - 1 < planes:
                pre = plus(pre, fine_conv(wide6, p + a - 1, weights, a))
        if p == 0:
            edge[0] = pre
        elif p == planes - 1:
            edge[1] = pre
        else:
            act[p - 1], slope[p - 1] = fine_finish(pre, half, fz)


def fine_outer(
    place, from_pair, from_next, weights, edge, act, halo6, pooled, slope, to_pair, to_next, sums
):
    half, fz = act.shape[1:3]
    coarse = pooled.shape[0]
    for e in range(2):
        fill_wide6(
            halo6,
            e,
            lambda y: facing(
                place,
                e,
                from_pair[2 * y : 2 * y + 2].reshape(1, fz, -1),
                from_next[2 * y : 2 * y + 2].reshape(1, fz, -1),
            ),
        )
        total, slope[e] = fine_finish(edge[e] + fine_conv(halo6, e, weights, 2 * e), half, fz)
        sums[e] = total + act[0 if e == 0 else 2 * coarse - 3]
    for pair in range(1, coarse - 1):
        sums[1 + pair] = act[2 * pair - 1] + act[2 * pair]
    for pair in range(coarse):
        at = 0 if pair == 0 else (1 if pair == coarse - 1 else 1 + pair)
        even = sums[at, :, pl.ds(0, fz // 2, stride=2), :]
        odd = sums[at, :, pl.ds(1, fz // 2, stride=2), :]
        pooled[pair] = ((even + odd) * 0.125).astype(BF16)
    last = coarse - 2
    for to, side in ((to_pair, 1 - place[0] % 2), (to_next, place[0] % 2)):
        for k in range(2):
            to[k] = pooled[side * last + k]


def coarse_conv(wide3, plane, kernel, a, total):
    cy, cz, span = (wide3.shape[1] - 2, wide3.shape[2], wide3.shape[3])
    rows = [wide3[plane, b : b + cy].reshape(cy * cz, span) for b in range(3)]
    return plus(total, dot(jnp.concatenate(rows, axis=1), kernel[a]))


def coarse_inner(own, kernel, wide3, pre):
    planes = own.shape[0]
    for p in range(planes):
        fill_wide3(wide3, p, own[p].astype(F32))
    for p in range(-1, planes + 1):
        total = None
        for a in range(3):
            if 0 <= p + a - 1 < planes:
                total = coarse_conv(wide3, p + a - 1, kernel, a, total)
        pre[p + 1] = total


def coarse_outer(
    place, from_pair, from_next, kernel, pre, cotangent, side_pair, side_next, halo3, out, delta
):
    planes, cy, cz, wide = cotangent.shape
    chan = from_pair.shape[-1]
    rows = side_pair.shape[0] - wide // chan * cy
    for e in range(2):
        for k in range(2):
            fill_wide3(halo3, 2 * e + k, facing(place, e, from_pair[k], from_next[k]))
    for p in range(-1, planes + 1):
        total = pre[p + 1]
        for a in range(3):
            at = p + a - 1
            if at < 0:
                total = coarse_conv(halo3, at + 2, kernel, a, total)
            elif at >= planes:
                total = coarse_conv(halo3, at - planes + 2, kernel, a, total)
        sig = jax.nn.sigmoid(total)
        if 0 <= p < planes:
            out[p] = (total * sig).astype(BF16).reshape(cy, cz, wide)
            grad = cotangent[p].reshape(cy * cz, wide).astype(F32)
        else:
            e = int(p >= planes)
            parts = []
            for k in range(wide // chan):
                lines = pl.ds(rows + k * cy, cy)
                parts.append(facing(place, e, side_pair[lines], side_next[lines]))
            grad = jnp.concatenate(parts, axis=-1).reshape(cy * cz, wide)
        grad = grad * silu_slope(total, sig)
        delta[p + 1] = grad.astype(BF16).reshape(cy, cz, wide)


def source(own, halo, plane):
    if plane < 0:
        return halo, 0
    if plane >= own.shape[0]:
        return halo, 1
    return own, plane


def put_term(term, lane, place, orders, keep, send):
    columns = pl.ds(lane, term.shape[1])
    if send is None:
        keep[:, columns] = term.astype(BF16)
        return
    here = place[0] % 2 == 0
    rows = term.shape[0] // (2 * len(orders))
    for at, owner in enumerate(orders):
        low = term[owner * rows : (owner + 1) * rows]
        high = term[(owner + 1) * rows : (owner + 2) * rows]
        keep[at, :, columns] = jnp.where(here, low, high).astype(BF16)
        send[at, :, columns] = jnp.where(here, high, low).astype(BF16)


def in_twos(taps):
    return [taps[k : k + 2] for k in range(0, len(taps), 2)]


def coarse_terms(place, wide3, halo3, delta, keep, send=None, *, order):
    planes, cy, cz, wide = delta.shape
    own = wide3.shape[0]
    span = wide3.shape[-1]

    def piece(p, tap):
        at = p + tap // 3 - 1
        ref = wide3 if 0 <= at < own else halo3
        at = at if 0 <= at < own else (1 if at < 0 else 2)
        return ref[at, tap % 3 : tap % 3 + cy].reshape(cy * cz, span)

    for group in in_twos(range(9)):
        total = None
        for p in range(own):
            pieces = jnp.concatenate([piece(p, tap) for tap in group], axis=1)
            total = plus(total, tap_dot(delta[p + 1].reshape(cy * cz, wide), pieces))
        put_term(total, group[0] * span, place, order, keep, send)


def fine_deltas(coarse_delta, kernel, slope, slope_edge, delta, wide3, spread):
    planes, cy, cz, wide = coarse_delta.shape
    chan = kernel.shape[1]
    for p in range(planes):
        fill_wide3(wide3, p, coarse_delta[p].astype(F32))
    grads = None
    for a in range(3):
        for b in range(3):
            for c in range(3):
                rows = wide3[a : a + planes - 2, b : b + cy, :, c * wide : (c + 1) * wide]
                term = lax.dot_general(
                    rows.reshape((planes - 2) * cy * cz, wide),
                    kernel[26 - (9 * a + 3 * b + c)],
                    (((1,), (1,)), ((), ())),
                    preferred_element_type=F32,
                )
                grads = plus(grads, term)
    for p in range(planes - 2):
        grad = grads[p * cy * cz : (p + 1) * cy * cz]
        grad = grad.astype(BF16).astype(F32).reshape(cy, cz, chan) * 0.125
        spread[:, pl.ds(0, cz, stride=2), :] = grad
        spread[:, pl.ds(1, cz, stride=2), :] = grad
        near = spread[...]
        both = jnp.concatenate([near, near], axis=-1)
        for at in range(2 * p, 2 * p + 2):
            ref, index = source(slope, slope_edge, at - 1)
            delta[at] = (both * ref[index].astype(F32)).astype(BF16)


def fine_terms(place, wide6, halo6, delta, keep, send=None, *, order, taps):
    planes, half, fz, double = delta.shape
    chan = double // 2
    three = 3 * chan

    def piece(p, q, tap):
        ref, at = source(wide6, halo6, p + tap // 3 - 1)
        pair, parity = ((q + tap % 3) // 2, (q + tap % 3) % 2)
        some = ref[at, pair : pair + half, :, parity * three : (parity + 1) * three]
        return some.reshape(half * fz, three)

    for group in in_twos(taps):
        total = None
        for p in range(planes):
            for q in range(2):
                rows = delta[p, :, :, q * chan : (q + 1) * chan].reshape(half * fz, chan)
                pieces = jnp.concatenate([piece(p, q, tap) for tap in group], axis=1)
                total = plus(total, tap_dot(rows, pieces))
        put_term(total, (group[0] - taps[0]) * three, place, order, keep, send)


def swap(value, bit):
    count = lax.axis_size("space")
    return lax.ppermute(value, "space", [(i, i ^ bit) for i in range(count)])


def swap_sample(value, bit=0):
    count = lax.axis_size("space")
    return lax.ppermute(
        value,
        ("sample", "space"),
        [(s * count + i, (1 - s) * count + (i ^ bit)) for s in range(2) for i in range(count)],
    )


def exchange_groups(count):
    bits = [1 << k for k in range(1, count.bit_length() - 2)]
    return [bits[k : k + 2] for k in range(0, len(bits), 2)]


def exchange_bits(count):
    return [bit for group in exchange_groups(count) for bit in group] + [count // 2]


def owners_in_order(count):
    bits = exchange_bits(count)
    return [
        sum(bit for k, bit in enumerate(bits) if at >> (len(bits) - 1 - k) & 1)
        for at in range(count // 2)
    ]


def term_shapes(rows, columns, count):
    owned = rows // count
    if owned % 8:
        return [jax.ShapeDtypeStruct((rows, columns), BF16)]
    return [jax.ShapeDtypeStruct((count // 2, owned, columns), BF16)] * 2


def pick(parts, bit):
    mine = lax.axis_index("space") // bit % 2
    keep = lax.dynamic_index_in_dim(parts, mine, 0, keepdims=False)
    return keep, lax.dynamic_index_in_dim(parts, 1 - mine, 0, keepdims=False)


def sided(terms, count):
    if len(terms) == 2:
        return terms
    bits = count.bit_length() - 1
    parts = terms[0].reshape((2,) * bits + (terms[0].shape[0] // count, -1))
    axes = [bits - bit.bit_length() for bit in [1] + exchange_bits(count)]
    sides = pick(parts.transpose(tuple(axes) + (bits, bits + 1)), 1)
    return [side.reshape((-1,) + side.shape[-2:]) for side in sides]


def masks_of(group):
    return [sum(bit for k, bit in enumerate(group) if turn >> k & 1) for turn in range(1 << len(group))]


def fold_body(place, *refs, group, chunks):
    pieces, outs = (refs[: sum(chunks)], refs[sum(chunks) :])
    span = outs[0].shape[0]
    lane = start = 0
    for length in chunks:
        some = pieces[start : start + length]
        columns = pl.ds(lane, some[0].shape[2])
        for mask, out in zip(masks_of(group), outs):
            at = 0
            for bit in group:
                mine = place[0] // bit % 2
                at = 2 * at + (1 - mine if mask & bit else mine)
            for k in range(span):
                total = None
                for piece in some:
                    total = plus(total, piece[at * span + k].astype(F32))
                out[k, :, columns] = total.astype(out.dtype)
        start += length
        lane += some[0].shape[2]


def fold(place, chunks, group, after=()):
    length, owned = chunks[0][0].shape[:2]
    extents = (length >> len(group), owned, sum(some[0].shape[2] for some in chunks))
    masks = masks_of(group)
    kept, *sends = kernel_call(
        functools.partial(fold_body, group=group, chunks=[len(some) for some in chunks]),
        [place] + [piece for some in chunks for piece in some],
        [jax.ShapeDtypeStruct(extents, BF16 if mask else F32) for mask in masks],
        [],
        0,
        8,
        scalars=1,
        after=after,
    )
    return dict(zip(masks[1:], sends)), kept


def received(sends, kept):
    return [kept] + [swap(part, mask) for mask, part in sends.items()]


def last_sum(sends, kept):
    bit = lax.axis_size("space") // 2
    base = (kept[0] + swap(sends[bit][0], bit).astype(F32)).astype(BF16)
    if lax.axis_size("sample") != 2:
        return lax.psum(base, "sample").astype(F32)
    return base.astype(F32) + swap_sample(base).astype(F32)


def last_direct(sends, kept):
    if lax.axis_size("sample") != 2:
        return last_sum(sends, kept)
    bit = lax.axis_size("space") // 2
    keep, send = (kept[0].astype(BF16), sends[bit][0])
    near, cross, other = (swap(send, bit), swap_sample(send, bit), swap_sample(keep))
    return (keep.astype(F32) + other.astype(F32)) + (near.astype(F32) + cross.astype(F32))


def shards(volumes, fine_kernel, coarse_kernel, cotangent):
    planes, fy, fz, chan = volumes.shape[1:]
    wide = coarse_kernel.shape[2]
    cp, cy, cz = (planes // 2, fy // 2, fz // 2)
    half = fy // 2
    count = lax.axis_size("space")
    me = lax.axis_index("space")
    parity = me % 2
    place = jnp.reshape(me, (1,)).astype(jnp.int32)
    x = volumes[0]
    cells, few = (planes * fy * fz, cp * cy * cz)
    fine_flops, coarse_flops = (54 * cells * chan * chan, 54 * few * chan * wide)

    def shape(*extents, kind=BF16):
        return jax.ShapeDtypeStruct(extents, kind)

    lines = 2 * fy + wide // chan * cy
    anywhere = pl.BlockSpec(memory_space=pl.ANY)
    to_pair, to_next = pl.pallas_call(
        side_planes,
        out_shape=[shape(lines, cz, chan)] * 2,
        in_specs=[SMEM, anywhere, anywhere],
        out_specs=[anywhere] * 2,
        scratch_shapes=[pltpu.SemaphoreType.DMA((2 + 2 * (wide // chan),))],
        cost_estimate=pl.CostEstimate(flops=fine_flops, bytes_accessed=2**20, transcendentals=0),
        compiler_params=pltpu.CompilerParams(vmem_limit_bytes=FETCH * 2**20),
    )(place, x.reshape(planes, 2 * fy, cz, chan), cotangent[0])
    side_pair, side_next = exchange(to_pair, to_next)
    mid = max(planes - 2, 1)
    wide6, weights, edge, act, slope = kernel_call(
        fine_inner,
        [x, fine_kernel.reshape(9, 3 * chan, chan)],
        [
            shape(planes, half + 1, fz, 6 * chan),
            shape(3, 2, 6 * chan, 2 * chan),
            shape(2, half * fz, 2 * chan, kind=F32),
            shape(mid, half, fz, chan, kind=F32),
            shape(mid, half, fz, 2 * chan),
        ],
        [],
        fine_flops,
        16,
    )
    halo6, pooled, slope_edge, to_pair, to_next = kernel_call(
        fine_outer,
        [place, side_pair, side_next, weights, edge, act],
        [
            shape(2, half + 1, fz, 6 * chan),
            shape(cp, cy, cz, chan),
            shape(2, half, fz, 2 * chan),
            shape(2, cy, cz, chan),
            shape(2, cy, cz, chan),
        ],
        [pltpu.VMEM((max(cp, 2), half, fz, chan), F32)],
        fine_flops // 6,
        16,
        scalars=1,
    )
    from_pair, from_next = exchange(to_pair, to_next)
    taps = coarse_kernel.reshape(3, 9 * chan, wide)
    wide3, pre = kernel_call(
        coarse_inner,
        [pooled, taps],
        [shape(cp, cy + 2, cz, 3 * chan), shape(cp + 2, cy * cz, wide, kind=F32)],
        [],
        coarse_flops,
        16,
    )
    halo3, out, coarse_delta = kernel_call(
        coarse_outer,
        [place, from_pair, from_next, taps, pre, cotangent[0], side_pair, side_next],
        [
            shape(4, cy + 2, cz, 3 * chan),
            shape(cp, cy, cz, wide),
            shape(cp + 2, cy, cz, wide),
        ],
        [],
        coarse_flops,
        16,
        scalars=1,
    )
    order = owners_in_order(count)
    steps = exchange_groups(count) + [[count // 2]]
    terms = kernel_call(
        functools.partial(coarse_terms, order=order),
        [place, wide3, halo3, coarse_delta],
        term_shapes(wide, 27 * chan, count),
        [],
        coarse_flops,
        16,
        scalars=1,
    )
    keep, send = sided(terms, count)
    early, coarse_kept = fold(place, [[keep, swap(send, 1)]], steps[0])
    (fine_delta,) = kernel_call(
        fine_deltas,
        [coarse_delta, coarse_kernel, slope, slope_edge],
        [shape(planes, half, fz, 2 * chan)],
        [pltpu.VMEM((cp + 2, cy + 2, cz, 3 * wide), BF16), pltpu.VMEM((cy, fz, chan), F32)],
        coarse_flops,
        16,
        after=[terms[-1]],
    )
    fine_parts = []
    before = list(early.values())[:1]
    for part in PARTS:
        fine_parts.append(
            kernel_call(
                functools.partial(fine_terms, order=order, taps=part),
                [place, wide6, halo6, fine_delta],
                term_shapes(chan, len(part) * 3 * chan, count),
                [],
                fine_flops // 3,
                16,
                scalars=1,
                after=before,
            )
        )
        before = [fine_parts[-1][-1]]
    got = received(early, coarse_kept)
    pieces = []
    for part in fine_parts:
        keep, send = sided(part, count)
        pieces.append([keep, swap(send, 1)])
    late, fine_kept = fold(place, pieces, steps[0], got[1:])
    for group in steps[1:]:
        early, coarse_kept = fold(place, [got], group, [late[steps[0][0]]])
        got = received(early, coarse_kept)
    coarse_grad = last_sum(early, coarse_kept)
    for group in steps[1:]:
        late, fine_kept = fold(place, [received(late, fine_kept)], group)
    fine_grad = last_direct(late, fine_kept)
    return (out[None], fine_grad, coarse_grad)


def solution(mesh):
    placed = (
        P("sample", "space", None, None, None),
        P(),
        P(),
        P("sample", "space", None, None, None),
    )
    return jax.shard_map(
        shards,
        mesh=mesh,
        in_specs=placed,
        out_specs=(P("sample", "space", None, None, None), P("space", None), P("space", None)),
        check_vma=False,
    )
```

```python
import functools

import jax
import jax.numpy as jnp
from jax import lax
from jax.experimental import pallas as pl
from jax.experimental.pallas import tpu as pltpu
from jax.sharding import PartitionSpec as P

F32 = jnp.float32
BF16 = jnp.bfloat16
COST = 64
SMALL = 50
PARTS = (range(0, 2), range(2, 6), range(6, 9))
VMEM = pl.BlockSpec(memory_space=pltpu.VMEM)
SMEM = pl.BlockSpec(memory_space=pltpu.SMEM)


def kernel_call(body, operands, outs, scratch, flops, limit, scalars=0, after=()):
    cost = pl.CostEstimate(flops=flops // COST, bytes_accessed=2**20, transcendentals=0)
    used, extra = (len(operands), len(after))
    specs = [SMEM] * scalars + [VMEM] * (used - scalars + extra)

    def inner(*refs):
        body(*refs[:used], *refs[used + extra :])

    return pl.pallas_call(
        inner,
        out_shape=outs,
        in_specs=specs,
        out_specs=[VMEM] * len(outs),
        scratch_shapes=scratch,
        cost_estimate=cost,
        compiler_params=pltpu.CompilerParams(vmem_limit_bytes=limit * 2**20),
    )(*operands, *after)


def exchange(to_pair, to_next):
    count = lax.axis_size("space")
    pair = [(i, i ^ 1) for i in range(count) if i ^ 1 < count]
    odd = [i for i in range(1, count - 1, 2)]
    across = [(i, i + 1) for i in odd] + [(i + 1, i) for i in odd]
    return lax.ppermute(to_pair, "space", pair), lax.ppermute(to_next, "space", across)


def silu_slope(value, sig):
    return sig * (1.0 + value * (1.0 - sig))


def three_shifts(value):
    depth = value.shape[1]
    at = lax.broadcasted_iota(jnp.int32, value.shape, 1)
    lower = jnp.where(at == 0, 0.0, pltpu.roll(value, 1, 1))
    upper = jnp.where(at == depth - 1, 0.0, pltpu.roll(value, depth - 1, 1))
    return lower, value, upper


def facing(place, edge, from_pair, from_next):
    return jnp.where(place[0] % 2 != edge, from_pair.astype(F32), from_next.astype(F32))


def dot(left, right):
    return jnp.dot(left, right, preferred_element_type=F32)


def tap_dot(left, right):
    return lax.dot_general(left, right, (((0,), (0,)), ((), ())), preferred_element_type=F32)


def plus(total, term):
    return term if total is None else total + term


def fill_wide6(target, plane, row_of):
    half = target.shape[1] - 1
    depth, lanes = target.shape[2:]
    three = lanes // 2
    zero = jnp.zeros((depth, three), BF16)
    target[plane, 0, :, 0:three] = zero
    target[plane, half, :, three:lanes] = zero
    for y in range(2 * half):
        pair, parity = ((y + 1) // 2, (y + 1) % 2)
        for c, piece in enumerate(three_shifts(row_of(y))):
            lane = parity * three + c * (three // 3)
            target[plane, pair : pair + 1, :, lane : lane + three // 3] = piece.astype(BF16)


def fill_wide3(target, plane, value):
    rows, depth, chan = value.shape
    zero = jnp.zeros((depth, 3 * chan), BF16)
    target[plane, 0] = zero
    target[plane, rows + 1] = zero
    for c, piece in enumerate(three_shifts(value)):
        target[plane, 1 : rows + 1, :, c * chan : (c + 1) * chan] = piece.astype(BF16)


def fine_conv(wide6, plane, weights, a):
    half = wide6.shape[1] - 1
    total = None
    for s in range(2):
        rows = wide6[plane, s : s + half].reshape(half * wide6.shape[2], wide6.shape[3])
        total = plus(total, dot(rows, weights[a, s]))
    return total


def fine_finish(pre, half, depth):
    chan = pre.shape[1] // 2
    sig = jax.nn.sigmoid(pre)
    act = (pre * sig).astype(BF16).astype(F32)
    slope = silu_slope(pre, sig).astype(BF16).reshape(half, depth, 2 * chan)
    return (act[:, :chan] + act[:, chan:]).reshape(half, depth, chan), slope


def side_planes(place, volume, to_pair, to_next, sems):
    last = volume.shape[0] - 1
    copies = [
        pltpu.make_async_copy(volume.at[(1 - place[0] % 2) * last], to_pair.at[0], sems.at[0]),
        pltpu.make_async_copy(volume.at[place[0] % 2 * last], to_next.at[0], sems.at[1]),
    ]
    for copy in copies:
        copy.start()
    for copy in copies:
        copy.wait()


def fine_inner(place, own, kernel, cotangent, wide6, weights, edge, act, slope, to_pair, to_next):
    planes, fy, fz, chan = own.shape
    half = fy // 2
    for s in range(2):
        for r in range(2):
            for q in range(2):
                b = 2 * s + r - q
                for a in range(3):
                    block = (a, s, pl.ds(r * 3 * chan, 3 * chan), pl.ds(q * chan, chan))
                    if 0 <= b <= 2:
                        weights[block] = kernel[3 * a + b]
                    else:
                        weights[block] = jnp.zeros((3 * chan, chan), BF16)
    last = cotangent.shape[0] - 1
    to_pair[0] = cotangent[(1 - place[0] % 2) * last]
    to_next[0] = cotangent[place[0] % 2 * last]
    done = 0
    for p in range(planes):
        while done < min(p + 2, planes):
            fill_wide6(wide6, done, lambda y: own[done, y : y + 1].astype(F32))
            done += 1
        pre = None
        for a in range(3):
            if 0 <= p + a - 1 < planes:
                pre = plus(pre, fine_conv(wide6, p + a - 1, weights, a))
        if p == 0:
            edge[0] = pre
        elif p == planes - 1:
            edge[1] = pre
        else:
            act[p - 1], slope[p - 1] = fine_finish(pre, half, fz)


def fine_outer(
    place, from_pair, from_next, weights, edge, act, halo6, pooled, slope, to_pair, to_next, sums
):
    half, fz = act.shape[1:3]
    coarse = pooled.shape[0]
    for e in range(2):
        fill_wide6(
            halo6,
            e,
            lambda y: facing(
                place,
                e,
                from_pair[0, y : y + 1],
                from_next[0, y : y + 1],
            ),
        )
        total, slope[e] = fine_finish(edge[e] + fine_conv(halo6, e, weights, 2 * e), half, fz)
        sums[e] = total + act[0 if e == 0 else 2 * coarse - 3]
    for pair in range(1, coarse - 1):
        sums[1 + pair] = act[2 * pair - 1] + act[2 * pair]
    for pair in range(coarse):
        at = 0 if pair == 0 else (1 if pair == coarse - 1 else 1 + pair)
        even = sums[at, :, pl.ds(0, fz // 2, stride=2), :]
        odd = sums[at, :, pl.ds(1, fz // 2, stride=2), :]
        pooled[pair] = ((even + odd) * 0.125).astype(BF16)
    last = coarse - 2
    for to, side in ((to_pair, 1 - place[0] % 2), (to_next, place[0] % 2)):
        for k in range(2):
            to[k] = pooled[side * last + k]


def coarse_conv(wide3, plane, kernel, a, total):
    cy, cz, span = (wide3.shape[1] - 2, wide3.shape[2], wide3.shape[3])
    rows = [wide3[plane, b : b + cy].reshape(cy * cz, span) for b in range(3)]
    return plus(total, dot(jnp.concatenate(rows, axis=1), kernel[a]))


def coarse_inner(own, kernel, wide3, pre):
    planes = own.shape[0]
    for p in range(planes):
        fill_wide3(wide3, p, own[p].astype(F32))
    for p in range(-1, planes + 1):
        total = None
        for a in range(3):
            if 0 <= p + a - 1 < planes:
                total = coarse_conv(wide3, p + a - 1, kernel, a, total)
        pre[p + 1] = total


def coarse_outer(
    place, from_pair, from_next, kernel, pre, cotangent, side_pair, side_next, halo3, out, delta
):
    planes, cy, cz, wide = cotangent.shape
    for e in range(2):
        for k in range(2):
            fill_wide3(halo3, 2 * e + k, facing(place, e, from_pair[k], from_next[k]))
    for p in range(-1, planes + 1):
        total = pre[p + 1]
        for a in range(3):
            at = p + a - 1
            if at < 0:
                total = coarse_conv(halo3, at + 2, kernel, a, total)
            elif at >= planes:
                total = coarse_conv(halo3, at - planes + 2, kernel, a, total)
        sig = jax.nn.sigmoid(total)
        if 0 <= p < planes:
            out[p] = (total * sig).astype(BF16).reshape(cy, cz, wide)
            grad = cotangent[p].reshape(cy * cz, wide).astype(F32)
        else:
            e = int(p >= planes)
            grad = facing(place, e, side_pair[0], side_next[0]).reshape(cy * cz, wide)
        grad = grad * silu_slope(total, sig)
        delta[p + 1] = grad.astype(BF16).reshape(cy, cz, wide)


def source(own, halo, plane):
    if plane < 0:
        return halo, 0
    if plane >= own.shape[0]:
        return halo, 1
    return own, plane


def put_term(term, lane, place, orders, keep, send):
    columns = pl.ds(lane, term.shape[1])
    if send is None:
        keep[:, columns] = term.astype(BF16)
        return
    here = place[0] % 2 == 0
    rows = term.shape[0] // (2 * len(orders))
    for at, owner in enumerate(orders):
        low = term[owner * rows : (owner + 1) * rows]
        high = term[(owner + 1) * rows : (owner + 2) * rows]
        keep[at, :, columns] = jnp.where(here, low, high).astype(BF16)
        send[at, :, columns] = jnp.where(here, high, low).astype(BF16)


def in_twos(taps):
    return [taps[k : k + 2] for k in range(0, len(taps), 2)]


def coarse_terms(place, wide3, halo3, delta, keep, send=None, *, order):
    planes, cy, cz, wide = delta.shape
    own = wide3.shape[0]
    span = wide3.shape[-1]

    def piece(p, tap):
        at = p + tap // 3 - 1
        ref = wide3 if 0 <= at < own else halo3
        at = at if 0 <= at < own else (1 if at < 0 else 2)
        return ref[at, tap % 3 : tap % 3 + cy].reshape(cy * cz, span)

    for group in in_twos(range(9)):
        total = None
        for p in range(own):
            pieces = jnp.concatenate([piece(p, tap) for tap in group], axis=1)
            total = plus(total, tap_dot(delta[p + 1].reshape(cy * cz, wide), pieces))
        put_term(total, group[0] * span, place, order, keep, send)


def fine_deltas(coarse_delta, kernel, slope, slope_edge, delta, wide3, spread):
    planes, cy, cz, wide = coarse_delta.shape
    chan = kernel.shape[1]
    for p in range(planes):
        fill_wide3(wide3, p, coarse_delta[p].astype(F32))
    grads = None
    for a in range(3):
        for b in range(3):
            for c in range(3):
                rows = wide3[a : a + planes - 2, b : b + cy, :, c * wide : (c + 1) * wide]
                term = lax.dot_general(
                    rows.reshape((planes - 2) * cy * cz, wide),
                    kernel[26 - (9 * a + 3 * b + c)],
                    (((1,), (1,)), ((), ())),
                    preferred_element_type=F32,
                )
                grads = plus(grads, term)
    for p in range(planes - 2):
        grad = grads[p * cy * cz : (p + 1) * cy * cz]
        grad = grad.astype(BF16).astype(F32).reshape(cy, cz, chan) * 0.125
        spread[:, pl.ds(0, cz, stride=2), :] = grad
        spread[:, pl.ds(1, cz, stride=2), :] = grad
        near = spread[...]
        both = jnp.concatenate([near, near], axis=-1)
        for at in range(2 * p, 2 * p + 2):
            ref, index = source(slope, slope_edge, at - 1)
            delta[at] = (both * ref[index].astype(F32)).astype(BF16)


def fine_terms(place, wide6, halo6, delta, keep, send=None, *, order, taps):
    planes, half, fz, double = delta.shape
    chan = double // 2
    three = 3 * chan

    def piece(p, q, tap):
        ref, at = source(wide6, halo6, p + tap // 3 - 1)
        pair, parity = ((q + tap % 3) // 2, (q + tap % 3) % 2)
        some = ref[at, pair : pair + half, :, parity * three : (parity + 1) * three]
        return some.reshape(half * fz, three)

    for group in in_twos(taps):
        total = None
        for p in range(planes):
            for q in range(2):
                rows = delta[p, :, :, q * chan : (q + 1) * chan].reshape(half * fz, chan)
                pieces = jnp.concatenate([piece(p, q, tap) for tap in group], axis=1)
                total = plus(total, tap_dot(rows, pieces))
        put_term(total, (group[0] - taps[0]) * three, place, order, keep, send)


def swap(value, bit):
    count = lax.axis_size("space")
    return lax.ppermute(value, "space", [(i, i ^ bit) for i in range(count)])


def swap_sample(value, bit=0):
    count = lax.axis_size("space")
    return lax.ppermute(
        value,
        ("sample", "space"),
        [(s * count + i, (1 - s) * count + (i ^ bit)) for s in range(2) for i in range(count)],
    )


def exchange_groups(count):
    bits = [1 << k for k in range(1, count.bit_length() - 2)]
    return [bits[k : k + 2] for k in range(0, len(bits), 2)]


def exchange_bits(count):
    return [bit for group in exchange_groups(count) for bit in group] + [count // 2]


def owners_in_order(count):
    bits = exchange_bits(count)
    return [
        sum(bit for k, bit in enumerate(bits) if at >> (len(bits) - 1 - k) & 1)
        for at in range(count // 2)
    ]


def term_shapes(rows, columns, count):
    owned = rows // count
    if owned % 8:
        return [jax.ShapeDtypeStruct((rows, columns), BF16)]
    return [jax.ShapeDtypeStruct((count // 2, owned, columns), BF16)] * 2


def pick(parts, bit):
    mine = lax.axis_index("space") // bit % 2
    keep = lax.dynamic_index_in_dim(parts, mine, 0, keepdims=False)
    return keep, lax.dynamic_index_in_dim(parts, 1 - mine, 0, keepdims=False)


def sided(terms, count):
    if len(terms) == 2:
        return terms
    bits = count.bit_length() - 1
    parts = terms[0].reshape((2,) * bits + (terms[0].shape[0] // count, -1))
    axes = [bits - bit.bit_length() for bit in [1] + exchange_bits(count)]
    sides = pick(parts.transpose(tuple(axes) + (bits, bits + 1)), 1)
    return [side.reshape((-1,) + side.shape[-2:]) for side in sides]


def masks_of(group):
    return [sum(bit for k, bit in enumerate(group) if turn >> k & 1) for turn in range(1 << len(group))]


def fold_body(place, *refs, group, chunks):
    pieces, outs = (refs[: sum(chunks)], refs[sum(chunks) :])
    span = outs[0].shape[0]
    lane = start = 0
    for length in chunks:
        some = pieces[start : start + length]
        columns = pl.ds(lane, some[0].shape[2])
        for mask, out in zip(masks_of(group), outs):
            at = 0
            for bit in group:
                mine = place[0] // bit % 2
                at = 2 * at + (1 - mine if mask & bit else mine)
            for k in range(span):
                total = None
                for piece in some:
                    total = plus(total, piece[at * span + k].astype(F32))
                out[k, :, columns] = total.astype(out.dtype)
        start += length
        lane += some[0].shape[2]


def fold(place, chunks, group, after=()):
    length, owned = chunks[0][0].shape[:2]
    extents = (length >> len(group), owned, sum(some[0].shape[2] for some in chunks))
    masks = masks_of(group)
    kept, *sends = kernel_call(
        functools.partial(fold_body, group=group, chunks=[len(some) for some in chunks]),
        [place] + [piece for some in chunks for piece in some],
        [jax.ShapeDtypeStruct(extents, BF16 if mask else F32) for mask in masks],
        [],
        0,
        8,
        scalars=1,
        after=after,
    )
    return dict(zip(masks[1:], sends)), kept


def received(sends, kept):
    return [kept] + [swap(part, mask) for mask, part in sends.items()]


def last_sum(sends, kept):
    bit = lax.axis_size("space") // 2
    base = (kept[0] + swap(sends[bit][0], bit).astype(F32)).astype(BF16)
    if lax.axis_size("sample") != 2:
        return lax.psum(base, "sample").astype(F32)
    return base.astype(F32) + swap_sample(base).astype(F32)


def last_direct(sends, kept):
    if lax.axis_size("sample") != 2:
        return last_sum(sends, kept)
    bit = lax.axis_size("space") // 2
    keep, send = (kept[0].astype(BF16), sends[bit][0])
    near, cross, other = (swap(send, bit), swap_sample(send, bit), swap_sample(keep))
    return (keep.astype(F32) + other.astype(F32)) + (near.astype(F32) + cross.astype(F32))


def shards(volumes, fine_kernel, coarse_kernel, cotangent):
    planes, fy, fz, chan = volumes.shape[1:]
    wide = coarse_kernel.shape[2]
    cp, cy, cz = (planes // 2, fy // 2, fz // 2)
    half = fy // 2
    count = lax.axis_size("space")
    me = lax.axis_index("space")
    parity = me % 2
    place = jnp.reshape(me, (1,)).astype(jnp.int32)
    x = volumes[0]
    cells, few = (planes * fy * fz, cp * cy * cz)
    fine_flops, coarse_flops = (54 * cells * chan * chan, 54 * few * chan * wide)

    def shape(*extents, kind=BF16):
        return jax.ShapeDtypeStruct(extents, kind)

    to_pair, to_next = pl.pallas_call(
        side_planes,
        out_shape=[shape(1, fy, fz, chan)] * 2,
        in_specs=[SMEM, pl.BlockSpec(memory_space=pl.ANY)],
        out_specs=[VMEM] * 2,
        scratch_shapes=[pltpu.SemaphoreType.DMA((2,))],
        cost_estimate=pl.CostEstimate(flops=fine_flops, bytes_accessed=2**20, transcendentals=0),
        compiler_params=pltpu.CompilerParams(vmem_limit_bytes=SMALL * 2**20),
    )(place, x)
    from_pair, from_next = exchange(to_pair, to_next)
    mid = max(planes - 2, 1)
    wide6, weights, edge, act, slope, to_pair, to_next = kernel_call(
        fine_inner,
        [place, x, fine_kernel.reshape(9, 3 * chan, chan), cotangent[0]],
        [
            shape(planes, half + 1, fz, 6 * chan),
            shape(3, 2, 6 * chan, 2 * chan),
            shape(2, half * fz, 2 * chan, kind=F32),
            shape(mid, half, fz, chan, kind=F32),
            shape(mid, half, fz, 2 * chan),
            shape(1, cy, cz, wide),
            shape(1, cy, cz, wide),
        ],
        [],
        fine_flops,
        16,
        scalars=1,
    )
    side_pair, side_next = exchange(to_pair, to_next)
    halo6, pooled, slope_edge, to_pair, to_next = kernel_call(
        fine_outer,
        [place, from_pair, from_next, weights, edge, act],
        [
            shape(2, half + 1, fz, 6 * chan),
            shape(cp, cy, cz, chan),
            shape(2, half, fz, 2 * chan),
            shape(2, cy, cz, chan),
            shape(2, cy, cz, chan),
        ],
        [pltpu.VMEM((max(cp, 2), half, fz, chan), F32)],
        fine_flops // 6,
        16,
        scalars=1,
    )
    from_pair, from_next = exchange(to_pair, to_next)
    taps = coarse_kernel.reshape(3, 9 * chan, wide)
    wide3, pre = kernel_call(
        coarse_inner,
        [pooled, taps],
        [shape(cp, cy + 2, cz, 3 * chan), shape(cp + 2, cy * cz, wide, kind=F32)],
        [],
        coarse_flops,
        16,
    )
    halo3, out, coarse_delta = kernel_call(
        coarse_outer,
        [place, from_pair, from_next, taps, pre, cotangent[0], side_pair, side_next],
        [
            shape(4, cy + 2, cz, 3 * chan),
            shape(cp, cy, cz, wide),
            shape(cp + 2, cy, cz, wide),
        ],
        [],
        coarse_flops,
        16,
        scalars=1,
    )
    order = owners_in_order(count)
    steps = exchange_groups(count) + [[count // 2]]
    terms = kernel_call(
        functools.partial(coarse_terms, order=order),
        [place, wide3, halo3, coarse_delta],
        term_shapes(wide, 27 * chan, count),
        [],
        coarse_flops,
        16,
        scalars=1,
    )
    keep, send = sided(terms, count)
    early, coarse_kept = fold(place, [[keep, swap(send, 1)]], steps[0])
    (fine_delta,) = kernel_call(
        fine_deltas,
        [coarse_delta, coarse_kernel, slope, slope_edge],
        [shape(planes, half, fz, 2 * chan)],
        [pltpu.VMEM((cp + 2, cy + 2, cz, 3 * wide), BF16), pltpu.VMEM((cy, fz, chan), F32)],
        coarse_flops,
        16,
        after=[terms[-1]],
    )
    fine_parts = []
    before = list(early.values())[:1]
    for part in PARTS:
        fine_parts.append(
            kernel_call(
                functools.partial(fine_terms, order=order, taps=part),
                [place, wide6, halo6, fine_delta],
                term_shapes(chan, len(part) * 3 * chan, count),
                [],
                fine_flops // 3,
                16,
                scalars=1,
                after=before,
            )
        )
        before = [fine_parts[-1][-1]]
    got = coarse_got = received(early, coarse_kept)
    pieces = []
    for part in fine_parts:
        keep, send = sided(part, count)
        pieces.append([keep, swap(send, 1)])
    late, fine_kept = fold(place, pieces, steps[0], coarse_got[1:])
    for group in steps[1:]:
        early, coarse_kept = fold(place, [got], group, [late[steps[0][0]]])
        got = received(early, coarse_kept)
    coarse_grad = last_sum(early, coarse_kept)
    for group in steps[1:]:
        late, fine_kept = fold(place, [received(late, fine_kept)], group)
    fine_grad = last_direct(late, fine_kept)
    return (out[None], fine_grad, coarse_grad)


def solution(mesh):
    placed = (
        P("sample", "space", None, None, None),
        P(),
        P(),
        P("sample", "space", None, None, None),
    )
    return jax.shard_map(
        shards,
        mesh=mesh,
        in_specs=placed,
        out_specs=(P("sample", "space", None, None, None), P("space", None), P("space", None)),
        check_vma=False,
    )
```

```python
import functools

import jax
import jax.numpy as jnp
from jax import lax
from jax.experimental import pallas as pl
from jax.experimental.pallas import tpu as pltpu
from jax.sharding import PartitionSpec as P

F32 = jnp.float32
BF16 = jnp.bfloat16
COST = 64
SPLIT = 4
SMALL = 50
VMEM = pl.BlockSpec(memory_space=pltpu.VMEM)
SMEM = pl.BlockSpec(memory_space=pltpu.SMEM)


def kernel_call(body, operands, outs, scratch, flops, limit, scalars=0, after=()):
    cost = pl.CostEstimate(flops=flops // COST, bytes_accessed=2**20, transcendentals=0)
    used, extra = (len(operands), len(after))
    specs = [SMEM] * scalars + [VMEM] * (used - scalars + extra)

    def inner(*refs):
        body(*refs[:used], *refs[used + extra :])

    return pl.pallas_call(
        inner,
        out_shape=outs,
        in_specs=specs,
        out_specs=[VMEM] * len(outs),
        scratch_shapes=scratch,
        cost_estimate=cost,
        compiler_params=pltpu.CompilerParams(vmem_limit_bytes=limit * 2**20),
    )(*operands, *after)


def exchange(to_pair, to_next):
    count = lax.axis_size("space")
    pair = [(i, i ^ 1) for i in range(count) if i ^ 1 < count]
    odd = [i for i in range(1, count - 1, 2)]
    across = [(i, i + 1) for i in odd] + [(i + 1, i) for i in odd]
    return lax.ppermute(to_pair, "space", pair), lax.ppermute(to_next, "space", across)


def silu_slope(value, sig):
    return sig * (1.0 + value * (1.0 - sig))


def three_shifts(value):
    depth = value.shape[1]
    at = lax.broadcasted_iota(jnp.int32, value.shape, 1)
    lower = jnp.where(at == 0, 0.0, pltpu.roll(value, 1, 1))
    upper = jnp.where(at == depth - 1, 0.0, pltpu.roll(value, depth - 1, 1))
    return lower, value, upper


def facing(place, edge, from_pair, from_next):
    return jnp.where(place[0] % 2 != edge, from_pair.astype(F32), from_next.astype(F32))


def dot(left, right):
    return jnp.dot(left, right, preferred_element_type=F32)


def tap_dot(left, right):
    return lax.dot_general(left, right, (((0,), (0,)), ((), ())), preferred_element_type=F32)


def plus(total, term):
    return term if total is None else total + term


def fill_wide6(target, plane, row_of):
    half = target.shape[1] - 1
    depth, lanes = target.shape[2:]
    three = lanes // 2
    zero = jnp.zeros((depth, three), BF16)
    target[plane, 0, :, 0:three] = zero
    target[plane, half, :, three:lanes] = zero
    for y in range(2 * half):
        pair, parity = ((y + 1) // 2, (y + 1) % 2)
        for c, piece in enumerate(three_shifts(row_of(y))):
            lane = parity * three + c * (three // 3)
            target[plane, pair : pair + 1, :, lane : lane + three // 3] = piece.astype(BF16)


def fill_wide3(target, plane, value):
    rows, depth, chan = value.shape
    zero = jnp.zeros((depth, 3 * chan), BF16)
    target[plane, 0] = zero
    target[plane, rows + 1] = zero
    for c, piece in enumerate(three_shifts(value)):
        target[plane, 1 : rows + 1, :, c * chan : (c + 1) * chan] = piece.astype(BF16)


def fine_conv(wide6, plane, weights, a):
    half = wide6.shape[1] - 1
    total = None
    for s in range(2):
        rows = wide6[plane, s : s + half].reshape(half * wide6.shape[2], wide6.shape[3])
        total = plus(total, dot(rows, weights[a, s]))
    return total


def fine_finish(pre, half, depth):
    chan = pre.shape[1] // 2
    sig = jax.nn.sigmoid(pre)
    act = (pre * sig).astype(BF16).astype(F32)
    slope = silu_slope(pre, sig).astype(BF16).reshape(half, depth, 2 * chan)
    return (act[:, :chan] + act[:, chan:]).reshape(half, depth, chan), slope


def side_planes(place, volume, to_pair, to_next, sems):
    last = volume.shape[0] - 1
    copies = [
        pltpu.make_async_copy(volume.at[(1 - place[0] % 2) * last], to_pair.at[0], sems.at[0]),
        pltpu.make_async_copy(volume.at[place[0] % 2 * last], to_next.at[0], sems.at[1]),
    ]
    for copy in copies:
        copy.start()
    for copy in copies:
        copy.wait()


def fine_inner(place, own, kernel, cotangent, wide6, weights, edge, act, slope, to_pair, to_next):
    planes, fy, fz, chan = own.shape
    half = fy // 2
    for s in range(2):
        for r in range(2):
            for q in range(2):
                b = 2 * s + r - q
                for a in range(3):
                    block = (a, s, pl.ds(r * 3 * chan, 3 * chan), pl.ds(q * chan, chan))
                    if 0 <= b <= 2:
                        weights[block] = kernel[3 * a + b]
                    else:
                        weights[block] = jnp.zeros((3 * chan, chan), BF16)
    last = cotangent.shape[0] - 1
    to_pair[0] = cotangent[(1 - place[0] % 2) * last]
    to_next[0] = cotangent[place[0] % 2 * last]
    done = 0
    for p in range(planes):
        while done < min(p + 2, planes):
            fill_wide6(wide6, done, lambda y: own[done, y : y + 1].astype(F32))
            done += 1
        pre = None
        for a in range(3):
            if 0 <= p + a - 1 < planes:
                pre = plus(pre, fine_conv(wide6, p + a - 1, weights, a))
        if p == 0:
            edge[0] = pre
        elif p == planes - 1:
            edge[1] = pre
        else:
            act[p - 1], slope[p - 1] = fine_finish(pre, half, fz)


def fine_outer(
    place, from_pair, from_next, weights, edge, act, halo6, pooled, slope, to_pair, to_next, sums
):
    half, fz = act.shape[1:3]
    coarse = pooled.shape[0]
    for e in range(2):
        fill_wide6(
            halo6,
            e,
            lambda y: facing(
                place,
                e,
                from_pair[0, y : y + 1],
                from_next[0, y : y + 1],
            ),
        )
        total, slope[e] = fine_finish(edge[e] + fine_conv(halo6, e, weights, 2 * e), half, fz)
        sums[e] = total + act[0 if e == 0 else 2 * coarse - 3]
    for pair in range(1, coarse - 1):
        sums[1 + pair] = act[2 * pair - 1] + act[2 * pair]
    for pair in range(coarse):
        at = 0 if pair == 0 else (1 if pair == coarse - 1 else 1 + pair)
        even = sums[at, :, pl.ds(0, fz // 2, stride=2), :]
        odd = sums[at, :, pl.ds(1, fz // 2, stride=2), :]
        pooled[pair] = ((even + odd) * 0.125).astype(BF16)
    last = coarse - 2
    for to, side in ((to_pair, 1 - place[0] % 2), (to_next, place[0] % 2)):
        for k in range(2):
            to[k] = pooled[side * last + k]


def coarse_conv(wide3, plane, kernel, a, total):
    cy, cz, span = (wide3.shape[1] - 2, wide3.shape[2], wide3.shape[3])
    rows = [wide3[plane, b : b + cy].reshape(cy * cz, span) for b in range(3)]
    return plus(total, dot(jnp.concatenate(rows, axis=1), kernel[a]))


def coarse_inner(own, kernel, wide3, pre):
    planes = own.shape[0]
    for p in range(planes):
        fill_wide3(wide3, p, own[p].astype(F32))
    for p in range(-1, planes + 1):
        total = None
        for a in range(3):
            if 0 <= p + a - 1 < planes:
                total = coarse_conv(wide3, p + a - 1, kernel, a, total)
        pre[p + 1] = total


def coarse_outer(
    place, from_pair, from_next, kernel, pre, cotangent, side_pair, side_next, halo3, out, delta
):
    planes, cy, cz, wide = cotangent.shape
    for e in range(2):
        for k in range(2):
            fill_wide3(halo3, 2 * e + k, facing(place, e, from_pair[k], from_next[k]))
    for p in range(-1, planes + 1):
        total = pre[p + 1]
        for a in range(3):
            at = p + a - 1
            if at < 0:
                total = coarse_conv(halo3, at + 2, kernel, a, total)
            elif at >= planes:
                total = coarse_conv(halo3, at - planes + 2, kernel, a, total)
        sig = jax.nn.sigmoid(total)
        if 0 <= p < planes:
            out[p] = (total * sig).astype(BF16).reshape(cy, cz, wide)
            grad = cotangent[p].reshape(cy * cz, wide).astype(F32)
        else:
            e = int(p >= planes)
            grad = facing(place, e, side_pair[0], side_next[0]).reshape(cy * cz, wide)
        grad = grad * silu_slope(total, sig)
        delta[p + 1] = grad.astype(BF16).reshape(cy, cz, wide)


def source(own, halo, plane):
    if plane < 0:
        return halo, 0
    if plane >= own.shape[0]:
        return halo, 1
    return own, plane


def put_term(term, lane, place, orders, keep, send):
    columns = pl.ds(lane, term.shape[1])
    if send is None:
        keep[:, columns] = term.astype(BF16)
        return
    here = place[0] % 2 == 0
    rows = term.shape[0] // (2 * len(orders))
    for at, owner in enumerate(orders):
        low = term[owner * rows : (owner + 1) * rows]
        high = term[(owner + 1) * rows : (owner + 2) * rows]
        keep[at, :, columns] = jnp.where(here, low, high).astype(BF16)
        send[at, :, columns] = jnp.where(here, high, low).astype(BF16)


def in_twos(taps):
    return [taps[k : k + 2] for k in range(0, len(taps), 2)]


def coarse_terms(place, wide3, halo3, delta, *outs, orders):
    planes, cy, cz, wide = delta.shape
    own = wide3.shape[0]
    span = wide3.shape[-1]

    def piece(p, tap):
        at = p + tap // 3 - 1
        ref = wide3 if 0 <= at < own else halo3
        at = at if 0 <= at < own else (1 if at < 0 else 2)
        return ref[at, tap % 3 : tap % 3 + cy].reshape(cy * cz, span)

    for group in in_twos(range(9)):
        total = None
        for p in range(own):
            pieces = jnp.concatenate([piece(p, tap) for tap in group], axis=1)
            total = plus(total, tap_dot(delta[p + 1].reshape(cy * cz, wide), pieces))
        for k, tap in enumerate(group):
            side = int(tap >= SPLIT)
            keep, send = outs[side], None
            if len(outs) == 4:
                keep, send = outs[2 * side : 2 * side + 2]
            term = total[:, k * span : (k + 1) * span]
            put_term(term, (tap - side * SPLIT) * span, place, orders[side], keep, send)


def fine_deltas(coarse_delta, kernel, slope, slope_edge, delta, wide3, spread):
    planes, cy, cz, wide = coarse_delta.shape
    chan = kernel.shape[1]
    for p in range(planes):
        fill_wide3(wide3, p, coarse_delta[p].astype(F32))
    grads = None
    for a in range(3):
        for b in range(3):
            for c in range(3):
                rows = wide3[a : a + planes - 2, b : b + cy, :, c * wide : (c + 1) * wide]
                term = lax.dot_general(
                    rows.reshape((planes - 2) * cy * cz, wide),
                    kernel[26 - (9 * a + 3 * b + c)],
                    (((1,), (1,)), ((), ())),
                    preferred_element_type=F32,
                )
                grads = plus(grads, term)
    for p in range(planes - 2):
        grad = grads[p * cy * cz : (p + 1) * cy * cz]
        grad = grad.astype(BF16).astype(F32).reshape(cy, cz, chan) * 0.125
        spread[:, pl.ds(0, cz, stride=2), :] = grad
        spread[:, pl.ds(1, cz, stride=2), :] = grad
        near = spread[...]
        both = jnp.concatenate([near, near], axis=-1)
        for at in range(2 * p, 2 * p + 2):
            ref, index = source(slope, slope_edge, at - 1)
            delta[at] = (both * ref[index].astype(F32)).astype(BF16)


def fine_terms(place, wide6, halo6, delta, *outs, order):
    planes, half, fz, double = delta.shape
    chan = double // 2
    three = 3 * chan

    def piece(p, q, tap):
        ref, at = source(wide6, halo6, p + tap // 3 - 1)
        pair, parity = ((q + tap % 3) // 2, (q + tap % 3) % 2)
        some = ref[at, pair : pair + half, :, parity * three : (parity + 1) * three]
        return some.reshape(half * fz, three)

    for group in in_twos(range(9)):
        total = None
        for p in range(planes):
            for q in range(2):
                rows = delta[p, :, :, q * chan : (q + 1) * chan].reshape(half * fz, chan)
                pieces = jnp.concatenate([piece(p, q, tap) for tap in group], axis=1)
                total = plus(total, tap_dot(rows, pieces))
        for k, tap in enumerate(group):
            keep, send = outs[tap // 3], None
            if len(outs) == 6:
                keep, send = outs[2 * (tap // 3) : 2 * (tap // 3) + 2]
            term = total[:, k * three : (k + 1) * three]
            put_term(term, tap % 3 * three, place, order, keep, send)


def swap(value, bit):
    count = lax.axis_size("space")
    return lax.ppermute(value, "space", [(i, i ^ bit) for i in range(count)])


def swap_sample(value, bit=0):
    count = lax.axis_size("space")
    return lax.ppermute(
        value,
        ("sample", "space"),
        [(s * count + i, (1 - s) * count + (i ^ bit)) for s in range(2) for i in range(count)],
    )


def exchange_groups(count):
    bits = [1 << k for k in range(1, count.bit_length() - 2)]
    return [bits[k : k + 2] for k in range(0, len(bits), 2)]


def exchange_bits(count):
    return [bit for group in exchange_groups(count) for bit in group] + [count // 2]


def owners_in_order(bits, count):
    return [
        sum(bit for k, bit in enumerate(bits) if at >> (len(bits) - 1 - k) & 1)
        for at in range(count // 2)
    ]


def term_shapes(rows, columns, count):
    owned = rows // count
    if owned % 8:
        return [jax.ShapeDtypeStruct((rows, columns), BF16)]
    return [jax.ShapeDtypeStruct((count // 2, owned, columns), BF16)] * 2


def pick(parts, bit):
    mine = lax.axis_index("space") // bit % 2
    keep = lax.dynamic_index_in_dim(parts, mine, 0, keepdims=False)
    return keep, lax.dynamic_index_in_dim(parts, 1 - mine, 0, keepdims=False)


def sided(terms, sequence, count):
    if len(terms) == 2:
        return terms
    bits = count.bit_length() - 1
    parts = terms[0].reshape((2,) * bits + (terms[0].shape[0] // count, -1))
    axes = [bits - bit.bit_length() for bit in [1] + sequence]
    sides = pick(parts.transpose(tuple(axes) + (bits, bits + 1)), 1)
    return [side.reshape((-1,) + side.shape[-2:]) for side in sides]


def masks_of(group):
    return [sum(bit for k, bit in enumerate(group) if turn >> k & 1) for turn in range(1 << len(group))]


def fold_body(place, *refs, group, chunks):
    pieces, outs = (refs[: sum(chunks)], refs[sum(chunks) :])
    span = outs[0].shape[0]
    lane = start = 0
    for length in chunks:
        some = pieces[start : start + length]
        columns = pl.ds(lane, some[0].shape[2])
        for mask, out in zip(masks_of(group), outs):
            at = 0
            for bit in group:
                mine = place[0] // bit % 2
                at = 2 * at + (1 - mine if mask & bit else mine)
            for k in range(span):
                total = None
                for piece in some:
                    total = plus(total, piece[at * span + k].astype(F32))
                out[k, :, columns] = total.astype(out.dtype)
        start += length
        lane += some[0].shape[2]


def fold(place, chunks, group, after=()):
    length, owned = chunks[0][0].shape[:2]
    extents = (length >> len(group), owned, sum(some[0].shape[2] for some in chunks))
    masks = masks_of(group)
    kept, *sends = kernel_call(
        functools.partial(fold_body, group=group, chunks=[len(some) for some in chunks]),
        [place] + [piece for some in chunks for piece in some],
        [jax.ShapeDtypeStruct(extents, BF16 if mask else F32) for mask in masks],
        [],
        0,
        8,
        scalars=1,
        after=after,
    )
    return dict(zip(masks[1:], sends)), kept


def received(sends, kept):
    return [kept] + [swap(part, mask) for mask, part in sends.items()]


def last_sum(sends, kept):
    bit = lax.axis_size("space") // 2
    base = (kept[0] + swap(sends[bit][0], bit).astype(F32)).astype(BF16)
    if lax.axis_size("sample") != 2:
        return lax.psum(base, "sample").astype(F32)
    return base.astype(F32) + swap_sample(base).astype(F32)


def last_direct(sends, kept):
    if lax.axis_size("sample") != 2:
        return last_sum(sends, kept)
    bit = lax.axis_size("space") // 2
    keep, send = (kept[0].astype(BF16), sends[bit][0])
    near, cross, other = (swap(send, bit), swap_sample(send, bit), swap_sample(keep))
    return (keep.astype(F32) + other.astype(F32)) + (near.astype(F32) + cross.astype(F32))


def pack_body(place, coarse_kept, coarse_got, *refs, bit):
    pieces, (send, both) = (refs[:-2], refs[-2:])
    mine = place[0] // bit % 2
    sums = []
    for side in (mine, 1 - mine):
        total = None
        for piece in pieces:
            total = plus(total, piece[side].astype(F32))
        sums.append(total)
    send[...] = sums[1].astype(BF16)
    coarse = coarse_kept[0] + coarse_got[0].astype(F32)
    both[...] = jnp.concatenate([coarse, sums[0]], axis=0).astype(BF16)


def result_body(both, other, near, cross, fine, coarse):
    total = both[...].astype(F32) + other[...].astype(F32)
    rows = coarse.shape[0]
    coarse[...] = total[:rows]
    fine[...] = total[rows:] + (near[...].astype(F32) + cross[...].astype(F32))


def last_together(place, coarse_early, coarse_kept, fine_pieces):
    bit = lax.axis_size("space") // 2
    coarse_got = swap(coarse_early[bit], bit)
    fine_rows, columns = fine_pieces[0].shape[1:]
    coarse_rows = coarse_kept.shape[1]
    shape = jax.ShapeDtypeStruct
    send, both = kernel_call(
        functools.partial(pack_body, bit=bit),
        [place, coarse_kept, coarse_got] + fine_pieces,
        [shape((fine_rows, columns), BF16), shape((coarse_rows + fine_rows, columns), BF16)],
        [],
        0,
        8,
        scalars=1,
    )
    near, cross, other = (swap(send, bit), swap_sample(send, bit), swap_sample(both))
    return kernel_call(
        result_body,
        [both, other, near, cross],
        [shape((fine_rows, columns), F32), shape((coarse_rows, columns), F32)],
        [],
        0,
        8,
    )


def shards(volumes, fine_kernel, coarse_kernel, cotangent):
    planes, fy, fz, chan = volumes.shape[1:]
    wide = coarse_kernel.shape[2]
    cp, cy, cz = (planes // 2, fy // 2, fz // 2)
    half = fy // 2
    count = lax.axis_size("space")
    me = lax.axis_index("space")
    parity = me % 2
    place = jnp.reshape(me, (1,)).astype(jnp.int32)
    x = volumes[0]
    cells, few = (planes * fy * fz, cp * cy * cz)
    fine_flops, coarse_flops = (54 * cells * chan * chan, 54 * few * chan * wide)

    def shape(*extents, kind=BF16):
        return jax.ShapeDtypeStruct(extents, kind)

    to_pair, to_next = pl.pallas_call(
        side_planes,
        out_shape=[shape(1, fy, fz, chan)] * 2,
        in_specs=[SMEM, pl.BlockSpec(memory_space=pl.ANY)],
        out_specs=[VMEM] * 2,
        scratch_shapes=[pltpu.SemaphoreType.DMA((2,))],
        cost_estimate=pl.CostEstimate(flops=fine_flops, bytes_accessed=2**20, transcendentals=0),
        compiler_params=pltpu.CompilerParams(vmem_limit_bytes=SMALL * 2**20),
    )(place, x)
    from_pair, from_next = exchange(to_pair, to_next)
    mid = max(planes - 2, 1)
    wide6, weights, edge, act, slope, to_pair, to_next = kernel_call(
        fine_inner,
        [place, x, fine_kernel.reshape(9, 3 * chan, chan), cotangent[0]],
        [
            shape(planes, half + 1, fz, 6 * chan),
            shape(3, 2, 6 * chan, 2 * chan),
            shape(2, half * fz, 2 * chan, kind=F32),
            shape(mid, half, fz, chan, kind=F32),
            shape(mid, half, fz, 2 * chan),
            shape(1, cy, cz, wide),
            shape(1, cy, cz, wide),
        ],
        [],
        fine_flops,
        16,
        scalars=1,
    )
    side_pair, side_next = exchange(to_pair, to_next)
    halo6, pooled, slope_edge, to_pair, to_next = kernel_call(
        fine_outer,
        [place, from_pair, from_next, weights, edge, act],
        [
            shape(2, half + 1, fz, 6 * chan),
            shape(cp, cy, cz, chan),
            shape(2, half, fz, 2 * chan),
            shape(2, cy, cz, chan),
            shape(2, cy, cz, chan),
        ],
        [pltpu.VMEM((max(cp, 2), half, fz, chan), F32)],
        fine_flops // 6,
        16,
        scalars=1,
    )
    from_pair, from_next = exchange(to_pair, to_next)
    taps = coarse_kernel.reshape(3, 9 * chan, wide)
    wide3, pre = kernel_call(
        coarse_inner,
        [pooled, taps],
        [shape(cp, cy + 2, cz, 3 * chan), shape(cp + 2, cy * cz, wide, kind=F32)],
        [],
        coarse_flops,
        16,
    )
    halo3, out, coarse_delta = kernel_call(
        coarse_outer,
        [place, from_pair, from_next, taps, pre, cotangent[0], side_pair, side_next],
        [
            shape(4, cy + 2, cz, 3 * chan),
            shape(cp, cy, cz, wide),
            shape(cp + 2, cy, cz, wide),
        ],
        [],
        coarse_flops,
        16,
        scalars=1,
    )
    bits = exchange_bits(count)
    order = owners_in_order(bits, count)
    steps = exchange_groups(count) + [[count // 2]]
    turned = [bit for group in steps for bit in reversed(group)]
    border = SPLIT * 3 * chan
    terms = kernel_call(
        functools.partial(
            coarse_terms, orders=(owners_in_order(bits, count), owners_in_order(turned, count))
        ),
        [place, wide3, halo3, coarse_delta],
        term_shapes(wide, border, count) + term_shapes(wide, 27 * chan - border, count),
        [],
        coarse_flops,
        16,
        scalars=1,
    )
    halves = []
    for side, sequence in enumerate((bits, turned)):
        some = terms[side * len(terms) // 2 : (side + 1) * len(terms) // 2]
        keep, send = sided(some, sequence, count)
        halves.append([keep, swap(send, 1)])
    sends = []
    if len(bits) > 1:
        for side, sequence in enumerate((bits, turned)):
            sends.append(fold(place, [halves[side]], sequence[:1]))
    early = [item for send, _ in sends for item in send.values()]
    (fine_delta,) = kernel_call(
        fine_deltas,
        [coarse_delta, coarse_kernel, slope, slope_edge],
        [shape(planes, half, fz, 2 * chan)],
        [pltpu.VMEM((cp + 2, cy + 2, cz, 3 * wide), BF16), pltpu.VMEM((cy, fz, chan), F32)],
        coarse_flops,
        16,
        after=[terms[-1]],
    )
    terms = kernel_call(
        functools.partial(fine_terms, order=order),
        [place, wide6, halo6, fine_delta],
        term_shapes(chan, 9 * chan, count) * 3,
        [],
        fine_flops,
        16,
        scalars=1,
        after=early,
    )
    each = len(terms) // 3
    fine_parts = [terms[k * each : (k + 1) * each] for k in range(3)]
    halves = [received(*send) for send in sends] or halves
    second = []
    for k in range(1, len(bits) - 1):
        sends = [fold(place, [halves[side]], [seq[k]]) for side, seq in enumerate((bits, turned))]
        second = second or [item for send, _ in sends for item in send.values()]
        halves = [received(*send) for send in sends]
    early, coarse_kept = fold(place, halves, bits[-1:])
    pieces = []
    for part in fine_parts:
        keep, send = sided(part, bits, count)
        pieces.append([keep, swap(send, 1)])
    late, fine_kept = fold(place, pieces, steps[0], second)
    for group in steps[1:-1]:
        late, fine_kept = fold(place, [received(late, fine_kept)], group)
    fine_got = received(late, fine_kept)
    if chan // count % 8 or lax.axis_size("sample") != 2:
        coarse_grad = last_sum(early, coarse_kept)
        fine_grad = last_direct(*fold(place, [fine_got], steps[-1]))
    else:
        fine_grad, coarse_grad = last_together(place, early, coarse_kept, fine_got)
    return (out[None], fine_grad, coarse_grad)


def solution(mesh):
    placed = (
        P("sample", "space", None, None, None),
        P(),
        P(),
        P("sample", "space", None, None, None),
    )
    return jax.shard_map(
        shards,
        mesh=mesh,
        in_specs=placed,
        out_specs=(P("sample", "space", None, None, None), P("space", None), P("space", None)),
        check_vma=False,
    )
```

```python
import functools

import jax
import jax.numpy as jnp
from jax import lax
from jax.experimental import pallas as pl
from jax.experimental.pallas import tpu as pltpu
from jax.sharding import PartitionSpec as P

F32 = jnp.float32
BF16 = jnp.bfloat16
COST = 64
SPLIT = 5
SMALL = 50
VMEM = pl.BlockSpec(memory_space=pltpu.VMEM)
SMEM = pl.BlockSpec(memory_space=pltpu.SMEM)


def kernel_call(body, operands, outs, scratch, flops, limit, scalars=0, after=()):
    cost = pl.CostEstimate(flops=flops // COST, bytes_accessed=2**20, transcendentals=0)
    used, extra = (len(operands), len(after))
    specs = [SMEM] * scalars + [VMEM] * (used - scalars + extra)

    def inner(*refs):
        body(*refs[:used], *refs[used + extra :])

    return pl.pallas_call(
        inner,
        out_shape=outs,
        in_specs=specs,
        out_specs=[VMEM] * len(outs),
        scratch_shapes=scratch,
        cost_estimate=cost,
        compiler_params=pltpu.CompilerParams(vmem_limit_bytes=limit * 2**20),
    )(*operands, *after)


def exchange(to_pair, to_next):
    count = lax.axis_size("space")
    pair = [(i, i ^ 1) for i in range(count) if i ^ 1 < count]
    odd = [i for i in range(1, count - 1, 2)]
    across = [(i, i + 1) for i in odd] + [(i + 1, i) for i in odd]
    return lax.ppermute(to_pair, "space", pair), lax.ppermute(to_next, "space", across)


def silu_slope(value, sig):
    return sig * (1.0 + value * (1.0 - sig))


def three_shifts(value):
    depth = value.shape[1]
    at = lax.broadcasted_iota(jnp.int32, value.shape, 1)
    lower = jnp.where(at == 0, 0.0, pltpu.roll(value, 1, 1))
    upper = jnp.where(at == depth - 1, 0.0, pltpu.roll(value, depth - 1, 1))
    return lower, value, upper


def facing(place, edge, from_pair, from_next):
    return jnp.where(place[0] % 2 != edge, from_pair.astype(F32), from_next.astype(F32))


def dot(left, right):
    return jnp.dot(left, right, preferred_element_type=F32)


def tap_dot(left, right):
    return lax.dot_general(left, right, (((0,), (0,)), ((), ())), preferred_element_type=F32)


def plus(total, term):
    return term if total is None else total + term


def fill_wide6(target, plane, row_of):
    half = target.shape[1] - 1
    depth, lanes = target.shape[2:]
    three = lanes // 2
    zero = jnp.zeros((depth, three), BF16)
    target[plane, 0, :, 0:three] = zero
    target[plane, half, :, three:lanes] = zero
    for y in range(2 * half):
        pair, parity = ((y + 1) // 2, (y + 1) % 2)
        for c, piece in enumerate(three_shifts(row_of(y))):
            lane = parity * three + c * (three // 3)
            target[plane, pair : pair + 1, :, lane : lane + three // 3] = piece.astype(BF16)


def fill_wide3(target, plane, value):
    rows, depth, chan = value.shape
    zero = jnp.zeros((depth, 3 * chan), BF16)
    target[plane, 0] = zero
    target[plane, rows + 1] = zero
    for c, piece in enumerate(three_shifts(value)):
        target[plane, 1 : rows + 1, :, c * chan : (c + 1) * chan] = piece.astype(BF16)


def fine_conv(wide6, plane, weights, a):
    half = wide6.shape[1] - 1
    total = None
    for s in range(2):
        rows = wide6[plane, s : s + half].reshape(half * wide6.shape[2], wide6.shape[3])
        total = plus(total, dot(rows, weights[a, s]))
    return total


def fine_finish(pre, half, depth):
    chan = pre.shape[1] // 2
    sig = jax.nn.sigmoid(pre)
    act = (pre * sig).astype(BF16).astype(F32)
    slope = silu_slope(pre, sig).astype(BF16).reshape(half, depth, 2 * chan)
    return (act[:, :chan] + act[:, chan:]).reshape(half, depth, chan), slope


def side_planes(place, volume, to_pair, to_next, sems):
    last = volume.shape[0] - 1
    copies = [
        pltpu.make_async_copy(volume.at[(1 - place[0] % 2) * last], to_pair.at[0], sems.at[0]),
        pltpu.make_async_copy(volume.at[place[0] % 2 * last], to_next.at[0], sems.at[1]),
    ]
    for copy in copies:
        copy.start()
    for copy in copies:
        copy.wait()


def fine_inner(place, own, kernel, cotangent, wide6, weights, edge, act, slope, to_pair, to_next):
    planes, fy, fz, chan = own.shape
    half = fy // 2
    for s in range(2):
        for r in range(2):
            for q in range(2):
                b = 2 * s + r - q
                for a in range(3):
                    block = (a, s, pl.ds(r * 3 * chan, 3 * chan), pl.ds(q * chan, chan))
                    if 0 <= b <= 2:
                        weights[block] = kernel[3 * a + b]
                    else:
                        weights[block] = jnp.zeros((3 * chan, chan), BF16)
    last = cotangent.shape[0] - 1
    to_pair[0] = cotangent[(1 - place[0] % 2) * last]
    to_next[0] = cotangent[place[0] % 2 * last]
    done = 0
    for p in range(planes):
        while done < min(p + 2, planes):
            fill_wide6(wide6, done, lambda y: own[done, y : y + 1].astype(F32))
            done += 1
        pre = None
        for a in range(3):
            if 0 <= p + a - 1 < planes:
                pre = plus(pre, fine_conv(wide6, p + a - 1, weights, a))
        if p == 0:
            edge[0] = pre
        elif p == planes - 1:
            edge[1] = pre
        else:
            act[p - 1], slope[p - 1] = fine_finish(pre, half, fz)


def fine_outer(
    place, from_pair, from_next, weights, edge, act, halo6, pooled, slope, to_pair, to_next, sums
):
    half, fz = act.shape[1:3]
    coarse = pooled.shape[0]
    for e in range(2):
        fill_wide6(
            halo6,
            e,
            lambda y: facing(
                place,
                e,
                from_pair[0, y : y + 1],
                from_next[0, y : y + 1],
            ),
        )
        total, slope[e] = fine_finish(edge[e] + fine_conv(halo6, e, weights, 2 * e), half, fz)
        sums[e] = total + act[0 if e == 0 else 2 * coarse - 3]
    for pair in range(1, coarse - 1):
        sums[1 + pair] = act[2 * pair - 1] + act[2 * pair]
    for pair in range(coarse):
        at = 0 if pair == 0 else (1 if pair == coarse - 1 else 1 + pair)
        even = sums[at, :, pl.ds(0, fz // 2, stride=2), :]
        odd = sums[at, :, pl.ds(1, fz // 2, stride=2), :]
        pooled[pair] = ((even + odd) * 0.125).astype(BF16)
    last = coarse - 2
    for to, side in ((to_pair, 1 - place[0] % 2), (to_next, place[0] % 2)):
        for k in range(2):
            to[k] = pooled[side * last + k]


def coarse_conv(wide3, plane, kernel, a, total):
    cy, cz, span = (wide3.shape[1] - 2, wide3.shape[2], wide3.shape[3])
    rows = [wide3[plane, b : b + cy].reshape(cy * cz, span) for b in range(3)]
    return plus(total, dot(jnp.concatenate(rows, axis=1), kernel[a]))


def coarse_inner(own, kernel, wide3, pre):
    planes = own.shape[0]
    for p in range(planes):
        fill_wide3(wide3, p, own[p].astype(F32))
    for p in range(-1, planes + 1):
        total = None
        for a in range(3):
            if 0 <= p + a - 1 < planes:
                total = coarse_conv(wide3, p + a - 1, kernel, a, total)
        pre[p + 1] = total


def coarse_outer(
    place, from_pair, from_next, kernel, pre, cotangent, side_pair, side_next, halo3, out, delta
):
    planes, cy, cz, wide = cotangent.shape
    for e in range(2):
        for k in range(2):
            fill_wide3(halo3, 2 * e + k, facing(place, e, from_pair[k], from_next[k]))
    for p in range(-1, planes + 1):
        total = pre[p + 1]
        for a in range(3):
            at = p + a - 1
            if at < 0:
                total = coarse_conv(halo3, at + 2, kernel, a, total)
            elif at >= planes:
                total = coarse_conv(halo3, at - planes + 2, kernel, a, total)
        sig = jax.nn.sigmoid(total)
        if 0 <= p < planes:
            out[p] = (total * sig).astype(BF16).reshape(cy, cz, wide)
            grad = cotangent[p].reshape(cy * cz, wide).astype(F32)
        else:
            e = int(p >= planes)
            grad = facing(place, e, side_pair[0], side_next[0]).reshape(cy * cz, wide)
        grad = grad * silu_slope(total, sig)
        delta[p + 1] = grad.astype(BF16).reshape(cy, cz, wide)


def source(own, halo, plane):
    if plane < 0:
        return halo, 0
    if plane >= own.shape[0]:
        return halo, 1
    return own, plane


def put_term(term, lane, place, orders, keep, send):
    columns = pl.ds(lane, term.shape[1])
    if send is None:
        keep[:, columns] = term.astype(BF16)
        return
    here = place[0] % 2 == 0
    rows = term.shape[0] // (2 * len(orders))
    for at, owner in enumerate(orders):
        low = term[owner * rows : (owner + 1) * rows]
        high = term[(owner + 1) * rows : (owner + 2) * rows]
        keep[at, :, columns] = jnp.where(here, low, high).astype(BF16)
        send[at, :, columns] = jnp.where(here, high, low).astype(BF16)


def in_twos(taps):
    return [taps[k : k + 2] for k in range(0, len(taps), 2)]


def coarse_terms(place, wide3, halo3, delta, *outs, orders):
    planes, cy, cz, wide = delta.shape
    own = wide3.shape[0]
    span = wide3.shape[-1]

    def piece(p, tap):
        at = p + tap // 3 - 1
        ref = wide3 if 0 <= at < own else halo3
        at = at if 0 <= at < own else (1 if at < 0 else 2)
        return ref[at, tap % 3 : tap % 3 + cy].reshape(cy * cz, span)

    for group in in_twos(range(9)):
        total = None
        for p in range(own):
            pieces = jnp.concatenate([piece(p, tap) for tap in group], axis=1)
            total = plus(total, tap_dot(delta[p + 1].reshape(cy * cz, wide), pieces))
        for k, tap in enumerate(group):
            side = int(tap >= SPLIT)
            keep, send = outs[side], None
            if len(outs) == 4:
                keep, send = outs[2 * side : 2 * side + 2]
            term = total[:, k * span : (k + 1) * span]
            put_term(term, (tap - side * SPLIT) * span, place, orders[side], keep, send)


def fine_deltas(coarse_delta, kernel, slope, slope_edge, delta, wide3, spread):
    planes, cy, cz, wide = coarse_delta.shape
    chan = kernel.shape[1]
    for p in range(planes):
        fill_wide3(wide3, p, coarse_delta[p].astype(F32))
    grads = None
    for a in range(3):
        for b in range(3):
            for c in range(3):
                rows = wide3[a : a + planes - 2, b : b + cy, :, c * wide : (c + 1) * wide]
                term = lax.dot_general(
                    rows.reshape((planes - 2) * cy * cz, wide),
                    kernel[26 - (9 * a + 3 * b + c)],
                    (((1,), (1,)), ((), ())),
                    preferred_element_type=F32,
                )
                grads = plus(grads, term)
    for p in range(planes - 2):
        grad = grads[p * cy * cz : (p + 1) * cy * cz]
        grad = grad.astype(BF16).astype(F32).reshape(cy, cz, chan) * 0.125
        spread[:, pl.ds(0, cz, stride=2), :] = grad
        spread[:, pl.ds(1, cz, stride=2), :] = grad
        near = spread[...]
        both = jnp.concatenate([near, near], axis=-1)
        for at in range(2 * p, 2 * p + 2):
            ref, index = source(slope, slope_edge, at - 1)
            delta[at] = (both * ref[index].astype(F32)).astype(BF16)


def fine_terms(place, wide6, halo6, delta, *outs, order):
    planes, half, fz, double = delta.shape
    chan = double // 2
    three = 3 * chan

    def piece(p, q, tap):
        ref, at = source(wide6, halo6, p + tap // 3 - 1)
        pair, parity = ((q + tap % 3) // 2, (q + tap % 3) % 2)
        some = ref[at, pair : pair + half, :, parity * three : (parity + 1) * three]
        return some.reshape(half * fz, three)

    for group in in_twos(range(9)):
        total = None
        for p in range(planes):
            for q in range(2):
                rows = delta[p, :, :, q * chan : (q + 1) * chan].reshape(half * fz, chan)
                pieces = jnp.concatenate([piece(p, q, tap) for tap in group], axis=1)
                total = plus(total, tap_dot(rows, pieces))
        for k, tap in enumerate(group):
            keep, send = outs[tap // 3], None
            if len(outs) == 6:
                keep, send = outs[2 * (tap // 3) : 2 * (tap // 3) + 2]
            term = total[:, k * three : (k + 1) * three]
            put_term(term, tap % 3 * three, place, order, keep, send)


def swap(value, bit):
    count = lax.axis_size("space")
    return lax.ppermute(value, "space", [(i, i ^ bit) for i in range(count)])


def swap_sample(value, bit=0):
    count = lax.axis_size("space")
    return lax.ppermute(
        value,
        ("sample", "space"),
        [(s * count + i, (1 - s) * count + (i ^ bit)) for s in range(2) for i in range(count)],
    )


def exchange_groups(count):
    bits = [1 << k for k in range(1, count.bit_length() - 2)]
    return [bits[k : k + 2] for k in range(0, len(bits), 2)]


def exchange_bits(count):
    return [bit for group in exchange_groups(count) for bit in group] + [count // 2]


def owners_in_order(bits, count):
    return [
        sum(bit for k, bit in enumerate(bits) if at >> (len(bits) - 1 - k) & 1)
        for at in range(count // 2)
    ]


def term_shapes(rows, columns, count):
    owned = rows // count
    if owned % 8:
        return [jax.ShapeDtypeStruct((rows, columns), BF16)]
    return [jax.ShapeDtypeStruct((count // 2, owned, columns), BF16)] * 2


def pick(parts, bit):
    mine = lax.axis_index("space") // bit % 2
    keep = lax.dynamic_index_in_dim(parts, mine, 0, keepdims=False)
    return keep, lax.dynamic_index_in_dim(parts, 1 - mine, 0, keepdims=False)


def sided(terms, sequence, count):
    if len(terms) == 2:
        return terms
    bits = count.bit_length() - 1
    parts = terms[0].reshape((2,) * bits + (terms[0].shape[0] // count, -1))
    axes = [bits - bit.bit_length() for bit in [1] + sequence]
    sides = pick(parts.transpose(tuple(axes) + (bits, bits + 1)), 1)
    return [side.reshape((-1,) + side.shape[-2:]) for side in sides]


def masks_of(group):
    return [sum(bit for k, bit in enumerate(group) if turn >> k & 1) for turn in range(1 << len(group))]


def fold_body(place, *refs, group, chunks):
    pieces, outs = (refs[: sum(chunks)], refs[sum(chunks) :])
    span = outs[0].shape[0]
    lane = start = 0
    for length in chunks:
        some = pieces[start : start + length]
        columns = pl.ds(lane, some[0].shape[2])
        for mask, out in zip(masks_of(group), outs):
            at = 0
            for bit in group:
                mine = place[0] // bit % 2
                at = 2 * at + (1 - mine if mask & bit else mine)
            for k in range(span):
                total = None
                for piece in some:
                    total = plus(total, piece[at * span + k].astype(F32))
                out[k, :, columns] = total.astype(out.dtype)
        start += length
        lane += some[0].shape[2]


def fold(place, chunks, group, after=()):
    length, owned = chunks[0][0].shape[:2]
    extents = (length >> len(group), owned, sum(some[0].shape[2] for some in chunks))
    masks = masks_of(group)
    kept, *sends = kernel_call(
        functools.partial(fold_body, group=group, chunks=[len(some) for some in chunks]),
        [place] + [piece for some in chunks for piece in some],
        [jax.ShapeDtypeStruct(extents, BF16 if mask else F32) for mask in masks],
        [],
        0,
        8,
        scalars=1,
        after=after,
    )
    return dict(zip(masks[1:], sends)), kept


def received(sends, kept):
    return [kept] + [swap(part, mask) for mask, part in sends.items()]


def last_sum(sends, kept):
    bit = lax.axis_size("space") // 2
    base = (kept[0] + swap(sends[bit][0], bit).astype(F32)).astype(BF16)
    if lax.axis_size("sample") != 2:
        return lax.psum(base, "sample").astype(F32)
    return base.astype(F32) + swap_sample(base).astype(F32)


def last_direct(sends, kept):
    if lax.axis_size("sample") != 2:
        return last_sum(sends, kept)
    bit = lax.axis_size("space") // 2
    keep, send = (kept[0].astype(BF16), sends[bit][0])
    near, cross, other = (swap(send, bit), swap_sample(send, bit), swap_sample(keep))
    return (keep.astype(F32) + other.astype(F32)) + (near.astype(F32) + cross.astype(F32))


def pack_body(place, coarse_kept, coarse_got, *refs, bit):
    pieces, (send, both) = (refs[:-2], refs[-2:])
    mine = place[0] // bit % 2
    sums = []
    for side in (mine, 1 - mine):
        total = None
        for piece in pieces:
            total = plus(total, piece[side].astype(F32))
        sums.append(total)
    send[...] = sums[1].astype(BF16)
    coarse = coarse_kept[0] + coarse_got[0].astype(F32)
    both[...] = jnp.concatenate([coarse, sums[0]], axis=0).astype(BF16)


def result_body(both, other, near, cross, fine, coarse):
    total = both[...].astype(F32) + other[...].astype(F32)
    rows = coarse.shape[0]
    coarse[...] = total[:rows]
    fine[...] = total[rows:] + (near[...].astype(F32) + cross[...].astype(F32))


def last_together(place, coarse_early, coarse_kept, fine_pieces):
    bit = lax.axis_size("space") // 2
    coarse_got = swap(coarse_early[bit], bit)
    fine_rows, columns = fine_pieces[0].shape[1:]
    coarse_rows = coarse_kept.shape[1]
    shape = jax.ShapeDtypeStruct
    send, both = kernel_call(
        functools.partial(pack_body, bit=bit),
        [place, coarse_kept, coarse_got] + fine_pieces,
        [shape((fine_rows, columns), BF16), shape((coarse_rows + fine_rows, columns), BF16)],
        [],
        0,
        8,
        scalars=1,
    )
    near, cross, other = (swap(send, bit), swap_sample(send, bit), swap_sample(both))
    return kernel_call(
        result_body,
        [both, other, near, cross],
        [shape((fine_rows, columns), F32), shape((coarse_rows, columns), F32)],
        [],
        0,
        8,
    )


def shards(volumes, fine_kernel, coarse_kernel, cotangent):
    planes, fy, fz, chan = volumes.shape[1:]
    wide = coarse_kernel.shape[2]
    cp, cy, cz = (planes // 2, fy // 2, fz // 2)
    half = fy // 2
    count = lax.axis_size("space")
    me = lax.axis_index("space")
    parity = me % 2
    place = jnp.reshape(me, (1,)).astype(jnp.int32)
    x = volumes[0]
    cells, few = (planes * fy * fz, cp * cy * cz)
    fine_flops, coarse_flops = (54 * cells * chan * chan, 54 * few * chan * wide)

    def shape(*extents, kind=BF16):
        return jax.ShapeDtypeStruct(extents, kind)

    to_pair, to_next = pl.pallas_call(
        side_planes,
        out_shape=[shape(1, fy, fz, chan)] * 2,
        in_specs=[SMEM, pl.BlockSpec(memory_space=pl.ANY)],
        out_specs=[VMEM] * 2,
        scratch_shapes=[pltpu.SemaphoreType.DMA((2,))],
        cost_estimate=pl.CostEstimate(flops=fine_flops, bytes_accessed=2**20, transcendentals=0),
        compiler_params=pltpu.CompilerParams(vmem_limit_bytes=SMALL * 2**20),
    )(place, x)
    from_pair, from_next = exchange(to_pair, to_next)
    mid = max(planes - 2, 1)
    wide6, weights, edge, act, slope, to_pair, to_next = kernel_call(
        fine_inner,
        [place, x, fine_kernel.reshape(9, 3 * chan, chan), cotangent[0]],
        [
            shape(planes, half + 1, fz, 6 * chan),
            shape(3, 2, 6 * chan, 2 * chan),
            shape(2, half * fz, 2 * chan, kind=F32),
            shape(mid, half, fz, chan, kind=F32),
            shape(mid, half, fz, 2 * chan),
            shape(1, cy, cz, wide),
            shape(1, cy, cz, wide),
        ],
        [],
        fine_flops,
        16,
        scalars=1,
    )
    side_pair, side_next = exchange(to_pair, to_next)
    halo6, pooled, slope_edge, to_pair, to_next = kernel_call(
        fine_outer,
        [place, from_pair, from_next, weights, edge, act],
        [
            shape(2, half + 1, fz, 6 * chan),
            shape(cp, cy, cz, chan),
            shape(2, half, fz, 2 * chan),
            shape(2, cy, cz, chan),
            shape(2, cy, cz, chan),
        ],
        [pltpu.VMEM((max(cp, 2), half, fz, chan), F32)],
        fine_flops // 6,
        16,
        scalars=1,
    )
    from_pair, from_next = exchange(to_pair, to_next)
    taps = coarse_kernel.reshape(3, 9 * chan, wide)
    wide3, pre = kernel_call(
        coarse_inner,
        [pooled, taps],
        [shape(cp, cy + 2, cz, 3 * chan), shape(cp + 2, cy * cz, wide, kind=F32)],
        [],
        coarse_flops,
        16,
    )
    halo3, out, coarse_delta = kernel_call(
        coarse_outer,
        [place, from_pair, from_next, taps, pre, cotangent[0], side_pair, side_next],
        [
            shape(4, cy + 2, cz, 3 * chan),
            shape(cp, cy, cz, wide),
            shape(cp + 2, cy, cz, wide),
        ],
        [],
        coarse_flops,
        16,
        scalars=1,
    )
    bits = exchange_bits(count)
    order = owners_in_order(bits, count)
    steps = exchange_groups(count) + [[count // 2]]
    turned = [bit for group in steps for bit in reversed(group)]
    border = SPLIT * 3 * chan
    terms = kernel_call(
        functools.partial(
            coarse_terms, orders=(owners_in_order(bits, count), owners_in_order(turned, count))
        ),
        [place, wide3, halo3, coarse_delta],
        term_shapes(wide, border, count) + term_shapes(wide, 27 * chan - border, count),
        [],
        coarse_flops,
        16,
        scalars=1,
    )
    (fine_delta,) = kernel_call(
        fine_deltas,
        [coarse_delta, coarse_kernel, slope, slope_edge],
        [shape(planes, half, fz, 2 * chan)],
        [pltpu.VMEM((cp + 2, cy + 2, cz, 3 * wide), BF16), pltpu.VMEM((cy, fz, chan), F32)],
        coarse_flops,
        16,
        after=[terms[-1]],
    )
    halves = []
    for side, sequence in enumerate((bits, turned)):
        some = terms[side * len(terms) // 2 : (side + 1) * len(terms) // 2]
        keep, send = sided(some, sequence, count)
        halves.append([keep, swap(send, 1)])
    sends = []
    if len(bits) > 1:
        for side, sequence in enumerate((bits, turned)):
            sends.append(fold(place, [halves[side]], sequence[:1], [fine_delta]))
    early = [item for send, _ in sends for item in send.values()]
    terms = kernel_call(
        functools.partial(fine_terms, order=order),
        [place, wide6, halo6, fine_delta],
        term_shapes(chan, 9 * chan, count) * 3,
        [],
        fine_flops,
        16,
        scalars=1,
        after=early,
    )
    each = len(terms) // 3
    fine_parts = [terms[k * each : (k + 1) * each] for k in range(3)]
    halves = [received(*send) for send in sends] or halves
    second = []
    for k in range(1, len(bits) - 1):
        sends = [fold(place, [halves[side]], [seq[k]]) for side, seq in enumerate((bits, turned))]
        second = second or [item for send, _ in sends for item in send.values()]
        halves = [received(*send) for send in sends]
    early, coarse_kept = fold(place, halves, bits[-1:])
    pieces = []
    for part in fine_parts:
        keep, send = sided(part, bits, count)
        pieces.append([keep, swap(send, 1)])
    late, fine_kept = fold(place, pieces, steps[0], second)
    for group in steps[1:-1]:
        late, fine_kept = fold(place, [received(late, fine_kept)], group)
    fine_got = received(late, fine_kept)
    if chan // count % 8 or lax.axis_size("sample") != 2:
        coarse_grad = last_sum(early, coarse_kept)
        fine_grad = last_direct(*fold(place, [fine_got], steps[-1]))
    else:
        fine_grad, coarse_grad = last_together(place, early, coarse_kept, fine_got)
    return (out[None], fine_grad, coarse_grad)


def solution(mesh):
    placed = (
        P("sample", "space", None, None, None),
        P(),
        P(),
        P("sample", "space", None, None, None),
    )
    return jax.shard_map(
        shards,
        mesh=mesh,
        in_specs=placed,
        out_specs=(P("sample", "space", None, None, None), P("space", None), P("space", None)),
        check_vma=False,
    )
```

```python
import functools

import jax
import jax.numpy as jnp
from jax import lax
from jax.experimental import pallas as pl
from jax.experimental.pallas import tpu as pltpu
from jax.sharding import PartitionSpec as P

F32 = jnp.float32
BF16 = jnp.bfloat16
COST = 64
SPLIT = 5
SMALL = 50
VMEM = pl.BlockSpec(memory_space=pltpu.VMEM)
SMEM = pl.BlockSpec(memory_space=pltpu.SMEM)


def kernel_call(body, operands, outs, scratch, flops, limit, scalars=0, after=()):
    cost = pl.CostEstimate(flops=flops // COST, bytes_accessed=2**20, transcendentals=0)
    used, extra = (len(operands), len(after))
    specs = [SMEM] * scalars + [VMEM] * (used - scalars + extra)

    def inner(*refs):
        body(*refs[:used], *refs[used + extra :])

    return pl.pallas_call(
        inner,
        out_shape=outs,
        in_specs=specs,
        out_specs=[VMEM] * len(outs),
        scratch_shapes=scratch,
        cost_estimate=cost,
        compiler_params=pltpu.CompilerParams(vmem_limit_bytes=limit * 2**20),
    )(*operands, *after)


def exchange(to_pair, to_next):
    count = lax.axis_size("space")
    pair = [(i, i ^ 1) for i in range(count) if i ^ 1 < count]
    odd = [i for i in range(1, count - 1, 2)]
    across = [(i, i + 1) for i in odd] + [(i + 1, i) for i in odd]
    return lax.ppermute(to_pair, "space", pair), lax.ppermute(to_next, "space", across)


def silu_slope(value, sig):
    return sig * (1.0 + value * (1.0 - sig))


def three_shifts(value):
    depth = value.shape[1]
    at = lax.broadcasted_iota(jnp.int32, value.shape, 1)
    lower = jnp.where(at == 0, 0.0, pltpu.roll(value, 1, 1))
    upper = jnp.where(at == depth - 1, 0.0, pltpu.roll(value, depth - 1, 1))
    return lower, value, upper


def facing(place, edge, from_pair, from_next):
    return jnp.where(place[0] % 2 != edge, from_pair.astype(F32), from_next.astype(F32))


def dot(left, right):
    return jnp.dot(left, right, preferred_element_type=F32)


def tap_dot(left, right):
    return lax.dot_general(left, right, (((0,), (0,)), ((), ())), preferred_element_type=F32)


def plus(total, term):
    return term if total is None else total + term


def fill_wide6(target, plane, row_of):
    half = target.shape[1] - 1
    depth, lanes = target.shape[2:]
    three = lanes // 2
    zero = jnp.zeros((depth, three), BF16)
    target[plane, 0, :, 0:three] = zero
    target[plane, half, :, three:lanes] = zero
    for y in range(2 * half):
        pair, parity = ((y + 1) // 2, (y + 1) % 2)
        for c, piece in enumerate(three_shifts(row_of(y))):
            lane = parity * three + c * (three // 3)
            target[plane, pair : pair + 1, :, lane : lane + three // 3] = piece.astype(BF16)


def fill_wide3(target, plane, value):
    rows, depth, chan = value.shape
    zero = jnp.zeros((depth, 3 * chan), BF16)
    target[plane, 0] = zero
    target[plane, rows + 1] = zero
    for c, piece in enumerate(three_shifts(value)):
        target[plane, 1 : rows + 1, :, c * chan : (c + 1) * chan] = piece.astype(BF16)


def fine_conv(wide6, plane, weights, a):
    half = wide6.shape[1] - 1
    total = None
    for s in range(2):
        rows = wide6[plane, s : s + half].reshape(half * wide6.shape[2], wide6.shape[3])
        total = plus(total, dot(rows, weights[a, s]))
    return total


def fine_finish(pre, half, depth):
    chan = pre.shape[1] // 2
    sig = jax.nn.sigmoid(pre)
    act = (pre * sig).astype(BF16).astype(F32)
    slope = silu_slope(pre, sig).astype(BF16).reshape(half, depth, 2 * chan)
    return (act[:, :chan] + act[:, chan:]).reshape(half, depth, chan), slope


def side_planes(place, volume, to_pair, to_next, sems):
    last = volume.shape[0] - 1
    copies = [
        pltpu.make_async_copy(volume.at[(1 - place[0] % 2) * last], to_pair.at[0], sems.at[0]),
        pltpu.make_async_copy(volume.at[place[0] % 2 * last], to_next.at[0], sems.at[1]),
    ]
    for copy in copies:
        copy.start()
    for copy in copies:
        copy.wait()


def fine_inner(place, own, kernel, cotangent, wide6, weights, edge, act, slope, to_pair, to_next):
    planes, fy, fz, chan = own.shape
    half = fy // 2
    for s in range(2):
        for r in range(2):
            for q in range(2):
                b = 2 * s + r - q
                for a in range(3):
                    block = (a, s, pl.ds(r * 3 * chan, 3 * chan), pl.ds(q * chan, chan))
                    if 0 <= b <= 2:
                        weights[block] = kernel[3 * a + b]
                    else:
                        weights[block] = jnp.zeros((3 * chan, chan), BF16)
    last = cotangent.shape[0] - 1
    to_pair[0] = cotangent[(1 - place[0] % 2) * last]
    to_next[0] = cotangent[place[0] % 2 * last]
    done = 0
    for p in range(planes):
        while done < min(p + 2, planes):
            fill_wide6(wide6, done, lambda y: own[done, y : y + 1].astype(F32))
            done += 1
        pre = None
        for a in range(3):
            if 0 <= p + a - 1 < planes:
                pre = plus(pre, fine_conv(wide6, p + a - 1, weights, a))
        if p == 0:
            edge[0] = pre
        elif p == planes - 1:
            edge[1] = pre
        else:
            act[p - 1], slope[p - 1] = fine_finish(pre, half, fz)


def fine_outer(
    place, from_pair, from_next, weights, edge, act, halo6, pooled, slope, to_pair, to_next, sums
):
    half, fz = act.shape[1:3]
    coarse = pooled.shape[0]
    for e in range(2):
        fill_wide6(
            halo6,
            e,
            lambda y: facing(
                place,
                e,
                from_pair[0, y : y + 1],
                from_next[0, y : y + 1],
            ),
        )
        total, slope[e] = fine_finish(edge[e] + fine_conv(halo6, e, weights, 2 * e), half, fz)
        sums[e] = total + act[0 if e == 0 else 2 * coarse - 3]
    for pair in range(1, coarse - 1):
        sums[1 + pair] = act[2 * pair - 1] + act[2 * pair]
    for pair in range(coarse):
        at = 0 if pair == 0 else (1 if pair == coarse - 1 else 1 + pair)
        even = sums[at, :, pl.ds(0, fz // 2, stride=2), :]
        odd = sums[at, :, pl.ds(1, fz // 2, stride=2), :]
        pooled[pair] = ((even + odd) * 0.125).astype(BF16)
    last = coarse - 2
    for to, side in ((to_pair, 1 - place[0] % 2), (to_next, place[0] % 2)):
        for k in range(2):
            to[k] = pooled[side * last + k]


def coarse_conv(wide3, plane, kernel, a, total):
    cy, cz, span = (wide3.shape[1] - 2, wide3.shape[2], wide3.shape[3])
    rows = [wide3[plane, b : b + cy].reshape(cy * cz, span) for b in range(3)]
    return plus(total, dot(jnp.concatenate(rows, axis=1), kernel[a]))


def coarse_inner(own, kernel, wide3, pre):
    planes = own.shape[0]
    for p in range(planes):
        fill_wide3(wide3, p, own[p].astype(F32))
    for p in range(-1, planes + 1):
        total = None
        for a in range(3):
            if 0 <= p + a - 1 < planes:
                total = coarse_conv(wide3, p + a - 1, kernel, a, total)
        pre[p + 1] = total


def coarse_outer(
    place, from_pair, from_next, kernel, pre, cotangent, side_pair, side_next, halo3, out, delta
):
    planes, cy, cz, wide = cotangent.shape
    for e in range(2):
        for k in range(2):
            fill_wide3(halo3, 2 * e + k, facing(place, e, from_pair[k], from_next[k]))
    for p in range(-1, planes + 1):
        total = pre[p + 1]
        for a in range(3):
            at = p + a - 1
            if at < 0:
                total = coarse_conv(halo3, at + 2, kernel, a, total)
            elif at >= planes:
                total = coarse_conv(halo3, at - planes + 2, kernel, a, total)
        sig = jax.nn.sigmoid(total)
        if 0 <= p < planes:
            out[p] = (total * sig).astype(BF16).reshape(cy, cz, wide)
            grad = cotangent[p].reshape(cy * cz, wide).astype(F32)
        else:
            e = int(p >= planes)
            grad = facing(place, e, side_pair[0], side_next[0]).reshape(cy * cz, wide)
        grad = grad * silu_slope(total, sig)
        delta[p + 1] = grad.astype(BF16).reshape(cy, cz, wide)


def source(own, halo, plane):
    if plane < 0:
        return halo, 0
    if plane >= own.shape[0]:
        return halo, 1
    return own, plane


def put_term(term, lane, place, orders, keep, send):
    columns = pl.ds(lane, term.shape[1])
    if send is None:
        keep[:, columns] = term.astype(BF16)
        return
    here = place[0] % 2 == 0
    rows = term.shape[0] // (2 * len(orders))
    for at, owner in enumerate(orders):
        low = term[owner * rows : (owner + 1) * rows]
        high = term[(owner + 1) * rows : (owner + 2) * rows]
        keep[at, :, columns] = jnp.where(here, low, high).astype(BF16)
        send[at, :, columns] = jnp.where(here, high, low).astype(BF16)


def in_twos(taps):
    return [taps[k : k + 2] for k in range(0, len(taps), 2)]


def coarse_terms(place, wide3, halo3, delta, *outs, orders):
    planes, cy, cz, wide = delta.shape
    own = wide3.shape[0]
    span = wide3.shape[-1]

    def piece(p, tap):
        at = p + tap // 3 - 1
        ref = wide3 if 0 <= at < own else halo3
        at = at if 0 <= at < own else (1 if at < 0 else 2)
        return ref[at, tap % 3 : tap % 3 + cy].reshape(cy * cz, span)

    for group in in_twos(range(9)):
        total = None
        for p in range(own):
            pieces = jnp.concatenate([piece(p, tap) for tap in group], axis=1)
            total = plus(total, tap_dot(delta[p + 1].reshape(cy * cz, wide), pieces))
        for k, tap in enumerate(group):
            side = int(tap >= SPLIT)
            keep, send = outs[side], None
            if len(outs) == 4:
                keep, send = outs[2 * side : 2 * side + 2]
            term = total[:, k * span : (k + 1) * span]
            put_term(term, (tap - side * SPLIT) * span, place, orders[side], keep, send)


def fine_deltas(coarse_delta, kernel, slope, slope_edge, delta, wide3, spread):
    planes, cy, cz, wide = coarse_delta.shape
    chan = kernel.shape[1]
    for p in range(planes):
        fill_wide3(wide3, p, coarse_delta[p].astype(F32))
    grads = None
    for a in range(3):
        for b in range(3):
            for c in range(3):
                rows = wide3[a : a + planes - 2, b : b + cy, :, c * wide : (c + 1) * wide]
                term = lax.dot_general(
                    rows.reshape((planes - 2) * cy * cz, wide),
                    kernel[26 - (9 * a + 3 * b + c)],
                    (((1,), (1,)), ((), ())),
                    preferred_element_type=F32,
                )
                grads = plus(grads, term)
    for p in range(planes - 2):
        grad = grads[p * cy * cz : (p + 1) * cy * cz]
        grad = grad.astype(BF16).astype(F32).reshape(cy, cz, chan) * 0.125
        spread[:, pl.ds(0, cz, stride=2), :] = grad
        spread[:, pl.ds(1, cz, stride=2), :] = grad
        near = spread[...]
        both = jnp.concatenate([near, near], axis=-1)
        for at in range(2 * p, 2 * p + 2):
            ref, index = source(slope, slope_edge, at - 1)
            delta[at] = (both * ref[index].astype(F32)).astype(BF16)


def fine_terms(place, wide6, halo6, delta, *outs, order):
    planes, half, fz, double = delta.shape
    chan = double // 2
    three = 3 * chan

    def piece(p, q, tap):
        ref, at = source(wide6, halo6, p + tap // 3 - 1)
        pair, parity = ((q + tap % 3) // 2, (q + tap % 3) % 2)
        some = ref[at, pair : pair + half, :, parity * three : (parity + 1) * three]
        return some.reshape(half * fz, three)

    for group in in_twos(range(9)):
        total = None
        for p in range(planes):
            for q in range(2):
                rows = delta[p, :, :, q * chan : (q + 1) * chan].reshape(half * fz, chan)
                pieces = jnp.concatenate([piece(p, q, tap) for tap in group], axis=1)
                total = plus(total, tap_dot(rows, pieces))
        for k, tap in enumerate(group):
            keep, send = outs[tap // 3], None
            if len(outs) == 6:
                keep, send = outs[2 * (tap // 3) : 2 * (tap // 3) + 2]
            term = total[:, k * three : (k + 1) * three]
            put_term(term, tap % 3 * three, place, order, keep, send)


def swap(value, bit):
    count = lax.axis_size("space")
    return lax.ppermute(value, "space", [(i, i ^ bit) for i in range(count)])


def swap_sample(value, bit=0):
    count = lax.axis_size("space")
    return lax.ppermute(
        value,
        ("sample", "space"),
        [(s * count + i, (1 - s) * count + (i ^ bit)) for s in range(2) for i in range(count)],
    )


def exchange_groups(count):
    bits = [1 << k for k in range(1, count.bit_length() - 2)]
    return [bits[k : k + 2] for k in range(0, len(bits), 2)]


def exchange_bits(count):
    return [bit for group in exchange_groups(count) for bit in group] + [count // 2]


def owners_in_order(bits, count):
    return [
        sum(bit for k, bit in enumerate(bits) if at >> (len(bits) - 1 - k) & 1)
        for at in range(count // 2)
    ]


def term_shapes(rows, columns, count):
    owned = rows // count
    if owned % 8:
        return [jax.ShapeDtypeStruct((rows, columns), BF16)]
    return [jax.ShapeDtypeStruct((count // 2, owned, columns), BF16)] * 2


def pick(parts, bit):
    mine = lax.axis_index("space") // bit % 2
    keep = lax.dynamic_index_in_dim(parts, mine, 0, keepdims=False)
    return keep, lax.dynamic_index_in_dim(parts, 1 - mine, 0, keepdims=False)


def sided(terms, sequence, count):
    if len(terms) == 2:
        return terms
    bits = count.bit_length() - 1
    parts = terms[0].reshape((2,) * bits + (terms[0].shape[0] // count, -1))
    axes = [bits - bit.bit_length() for bit in [1] + sequence]
    sides = pick(parts.transpose(tuple(axes) + (bits, bits + 1)), 1)
    return [side.reshape((-1,) + side.shape[-2:]) for side in sides]


def masks_of(group):
    return [sum(bit for k, bit in enumerate(group) if turn >> k & 1) for turn in range(1 << len(group))]


def fold_body(place, *refs, group, chunks):
    pieces, outs = (refs[: sum(chunks)], refs[sum(chunks) :])
    span = outs[0].shape[0]
    lane = start = 0
    for length in chunks:
        some = pieces[start : start + length]
        columns = pl.ds(lane, some[0].shape[2])
        for mask, out in zip(masks_of(group), outs):
            at = 0
            for bit in group:
                mine = place[0] // bit % 2
                at = 2 * at + (1 - mine if mask & bit else mine)
            for k in range(span):
                total = None
                for piece in some:
                    total = plus(total, piece[at * span + k].astype(F32))
                out[k, :, columns] = total.astype(out.dtype)
        start += length
        lane += some[0].shape[2]


def fold(place, chunks, group, after=()):
    length, owned = chunks[0][0].shape[:2]
    extents = (length >> len(group), owned, sum(some[0].shape[2] for some in chunks))
    masks = masks_of(group)
    kept, *sends = kernel_call(
        functools.partial(fold_body, group=group, chunks=[len(some) for some in chunks]),
        [place] + [piece for some in chunks for piece in some],
        [jax.ShapeDtypeStruct(extents, BF16 if mask else F32) for mask in masks],
        [],
        0,
        8,
        scalars=1,
        after=after,
    )
    return dict(zip(masks[1:], sends)), kept


def received(sends, kept):
    return [kept] + [swap(part, mask) for mask, part in sends.items()]


def last_sum(sends, kept):
    bit = lax.axis_size("space") // 2
    base = (kept[0] + swap(sends[bit][0], bit).astype(F32)).astype(BF16)
    if lax.axis_size("sample") != 2:
        return lax.psum(base, "sample").astype(F32)
    return base.astype(F32) + swap_sample(base).astype(F32)


def last_direct(sends, kept):
    if lax.axis_size("sample") != 2:
        return last_sum(sends, kept)
    bit = lax.axis_size("space") // 2
    keep, send = (kept[0].astype(BF16), sends[bit][0])
    near, cross, other = (swap(send, bit), swap_sample(send, bit), swap_sample(keep))
    return (keep.astype(F32) + other.astype(F32)) + (near.astype(F32) + cross.astype(F32))


def pack_body(place, coarse_kept, coarse_got, *refs, bit):
    pieces, (send, both) = (refs[:-2], refs[-2:])
    mine = place[0] // bit % 2
    sums = []
    for side in (mine, 1 - mine):
        total = None
        for piece in pieces:
            total = plus(total, piece[side].astype(F32))
        sums.append(total)
    send[...] = sums[1].astype(BF16)
    coarse = coarse_kept[0] + coarse_got[0].astype(F32)
    both[...] = jnp.concatenate([coarse, sums[0]], axis=0).astype(BF16)


def result_body(both, other, near, cross, fine, coarse):
    total = both[...].astype(F32) + other[...].astype(F32)
    rows = coarse.shape[0]
    coarse[...] = total[:rows]
    fine[...] = total[rows:] + (near[...].astype(F32) + cross[...].astype(F32))


def last_together(place, coarse_early, coarse_kept, fine_pieces):
    bit = lax.axis_size("space") // 2
    coarse_got = swap(coarse_early[bit], bit)
    fine_rows, columns = fine_pieces[0].shape[1:]
    coarse_rows = coarse_kept.shape[1]
    shape = jax.ShapeDtypeStruct
    send, both = kernel_call(
        functools.partial(pack_body, bit=bit),
        [place, coarse_kept, coarse_got] + fine_pieces,
        [shape((fine_rows, columns), BF16), shape((coarse_rows + fine_rows, columns), BF16)],
        [],
        0,
        8,
        scalars=1,
    )
    near, cross, other = (swap(send, bit), swap_sample(send, bit), swap_sample(both))
    return kernel_call(
        result_body,
        [both, other, near, cross],
        [shape((fine_rows, columns), F32), shape((coarse_rows, columns), F32)],
        [],
        0,
        8,
    )


def shards(volumes, fine_kernel, coarse_kernel, cotangent):
    planes, fy, fz, chan = volumes.shape[1:]
    wide = coarse_kernel.shape[2]
    cp, cy, cz = (planes // 2, fy // 2, fz // 2)
    half = fy // 2
    count = lax.axis_size("space")
    me = lax.axis_index("space")
    parity = me % 2
    place = jnp.reshape(me, (1,)).astype(jnp.int32)
    x = volumes[0]
    cells, few = (planes * fy * fz, cp * cy * cz)
    fine_flops, coarse_flops = (54 * cells * chan * chan, 54 * few * chan * wide)

    def shape(*extents, kind=BF16):
        return jax.ShapeDtypeStruct(extents, kind)

    to_pair, to_next = pl.pallas_call(
        side_planes,
        out_shape=[shape(1, fy, fz, chan)] * 2,
        in_specs=[SMEM, pl.BlockSpec(memory_space=pl.ANY)],
        out_specs=[VMEM] * 2,
        scratch_shapes=[pltpu.SemaphoreType.DMA((2,))],
        cost_estimate=pl.CostEstimate(flops=fine_flops, bytes_accessed=2**20, transcendentals=0),
        compiler_params=pltpu.CompilerParams(vmem_limit_bytes=SMALL * 2**20),
    )(place, x)
    from_pair, from_next = exchange(to_pair, to_next)
    mid = max(planes - 2, 1)
    wide6, weights, edge, act, slope, to_pair, to_next = kernel_call(
        fine_inner,
        [place, x, fine_kernel.reshape(9, 3 * chan, chan), cotangent[0]],
        [
            shape(planes, half + 1, fz, 6 * chan),
            shape(3, 2, 6 * chan, 2 * chan),
            shape(2, half * fz, 2 * chan, kind=F32),
            shape(mid, half, fz, chan, kind=F32),
            shape(mid, half, fz, 2 * chan),
            shape(1, cy, cz, wide),
            shape(1, cy, cz, wide),
        ],
        [],
        fine_flops,
        16,
        scalars=1,
    )
    side_pair, side_next = exchange(to_pair, to_next)
    halo6, pooled, slope_edge, to_pair, to_next = kernel_call(
        fine_outer,
        [place, from_pair, from_next, weights, edge, act],
        [
            shape(2, half + 1, fz, 6 * chan),
            shape(cp, cy, cz, chan),
            shape(2, half, fz, 2 * chan),
            shape(2, cy, cz, chan),
            shape(2, cy, cz, chan),
        ],
        [pltpu.VMEM((max(cp, 2), half, fz, chan), F32)],
        fine_flops // 6,
        16,
        scalars=1,
    )
    from_pair, from_next = exchange(to_pair, to_next)
    taps = coarse_kernel.reshape(3, 9 * chan, wide)
    wide3, pre = kernel_call(
        coarse_inner,
        [pooled, taps],
        [shape(cp, cy + 2, cz, 3 * chan), shape(cp + 2, cy * cz, wide, kind=F32)],
        [],
        coarse_flops,
        16,
    )
    halo3, out, coarse_delta = kernel_call(
        coarse_outer,
        [place, from_pair, from_next, taps, pre, cotangent[0], side_pair, side_next],
        [
            shape(4, cy + 2, cz, 3 * chan),
            shape(cp, cy, cz, wide),
            shape(cp + 2, cy, cz, wide),
        ],
        [],
        coarse_flops,
        16,
        scalars=1,
    )
    bits = exchange_bits(count)
    order = owners_in_order(bits, count)
    steps = exchange_groups(count) + [[count // 2]]
    turned = [bit for group in steps for bit in reversed(group)]
    border = SPLIT * 3 * chan
    terms = kernel_call(
        functools.partial(
            coarse_terms, orders=(owners_in_order(bits, count), owners_in_order(turned, count))
        ),
        [place, wide3, halo3, coarse_delta],
        term_shapes(wide, border, count) + term_shapes(wide, 27 * chan - border, count),
        [],
        coarse_flops,
        16,
        scalars=1,
    )
    (fine_delta,) = kernel_call(
        fine_deltas,
        [coarse_delta, coarse_kernel, slope, slope_edge],
        [shape(planes, half, fz, 2 * chan)],
        [pltpu.VMEM((cp + 2, cy + 2, cz, 3 * wide), BF16), pltpu.VMEM((cy, fz, chan), F32)],
        coarse_flops,
        16,
        after=[terms[-1]],
    )
    halves = []
    for side, sequence in enumerate((bits, turned)):
        some = terms[side * len(terms) // 2 : (side + 1) * len(terms) // 2]
        keep, send = sided(some, sequence, count)
        halves.append([keep, swap(send, 1)])
    sends = []
    if len(bits) > 1:
        for side, sequence in enumerate((bits, turned)):
            sends.append(fold(place, [halves[side]], sequence[:1], [fine_delta][:side]))
    early = [item for send, _ in sends for item in send.values()]
    terms = kernel_call(
        functools.partial(fine_terms, order=order),
        [place, wide6, halo6, fine_delta],
        term_shapes(chan, 9 * chan, count) * 3,
        [],
        fine_flops,
        16,
        scalars=1,
        after=early,
    )
    each = len(terms) // 3
    fine_parts = [terms[k * each : (k + 1) * each] for k in range(3)]
    halves = [received(*send) for send in sends] or halves
    second = []
    for k in range(1, len(bits) - 1):
        sends = [fold(place, [halves[side]], [seq[k]]) for side, seq in enumerate((bits, turned))]
        second = second or [item for send, _ in sends for item in send.values()]
        halves = [received(*send) for send in sends]
    early, coarse_kept = fold(place, halves, bits[-1:])
    pieces = []
    for part in fine_parts:
        keep, send = sided(part, bits, count)
        pieces.append([keep, swap(send, 1)])
    late, fine_kept = fold(place, pieces, steps[0], second)
    for group in steps[1:-1]:
        late, fine_kept = fold(place, [received(late, fine_kept)], group)
    fine_got = received(late, fine_kept)
    if chan // count % 8 or lax.axis_size("sample") != 2:
        coarse_grad = last_sum(early, coarse_kept)
        fine_grad = last_direct(*fold(place, [fine_got], steps[-1]))
    else:
        fine_grad, coarse_grad = last_together(place, early, coarse_kept, fine_got)
    return (out[None], fine_grad, coarse_grad)


def solution(mesh):
    placed = (
        P("sample", "space", None, None, None),
        P(),
        P(),
        P("sample", "space", None, None, None),
    )
    return jax.shard_map(
        shards,
        mesh=mesh,
        in_specs=placed,
        out_specs=(P("sample", "space", None, None, None), P("space", None), P("space", None)),
        check_vma=False,
    )
```
